32 devices in a mesh: horiz: 8 (over z, y), vert: 4 (over x, core).
Axes of the slice: x: 2, y: 2, z: 4, core: 2. Of those that a mesh axis runs over, the one named last changes fastest.
Arguments:
- tracer: bfloat16 [8, 2048, 128], P('vert', 'horiz'), may hold values from -6 to 6
- explicit_tiles: bfloat16 [8, 16, 7, 128, 128], P('vert', 'horiz'), may hold values from -0.25 to 0.25
- tile_columns: int32 [8, 16, 7], P('vert', 'horiz'), may hold values from 0 to 127, as said below
- tile_counts: int32 [8, 16], P('vert', 'horiz'), may hold values from 4 to 7
- surface_source: bfloat16 [2048, 128], P('horiz'), may hold values from -6 to 6
- implicit_columns: float32 [2048, 8, 8], P(('horiz', 'vert')), may hold values from -0.53033009 to 1
- settling: float32 [128], replicated, may hold values from 0.02 to 0.5
- wet_mask: int32 [8, 2048], P('vert', 'horiz'), may hold values 0 or 1
Outputs:
- tracer_out: bfloat16 [8, 2048, 128], P('vert', 'horiz')
The draws below stay inside these ranges and needn't reach their ends.
Inputs may be any that keep to these rules, and one draw needn't show every extreme that they name: `tile_columns`: slot 0 of block row (l, t) names the row's own tile l * 16 + t; the other slots name distinct tiles within 2 levels and 2 tiles of it, inside the grid.
All inputs are finite; a program needn't handle non-finite values. No bound on the sum of `wet_mask` on one device may be relied on, other than what follows from the above.
Results may differ from the reference program's by a relative error of at most 0.015.
Values may be sent and summed in bfloat16 or wider, within the bound.
A program may use at most 64 MiB of HBM per device.

```python
import math
import jax
import jax.numpy as jnp
from jax import lax

TILE = 128
CLASSES = 128
SLOTS = 7
REACH = 2
STEPS = 4
H_TILES = 16
H_CELLS = 2048
LEVELS = 8


def draw_tile_columns(key, part):
    side_width = 2 * REACH + 1
    candidate = jnp.arange(side_width * side_width, dtype=jnp.int32)
    level_step = candidate // side_width - REACH
    tile_step = candidate % side_width - REACH
    level_index = jnp.arange(LEVELS, dtype=jnp.int32)[:, None, None]
    tile_index = jnp.arange(H_TILES, dtype=jnp.int32)[None, :, None]
    full_shape = (LEVELS, H_TILES, side_width * side_width)
    near_level = jnp.broadcast_to(level_index + level_step[None, None, :], full_shape)
    near_tile = jnp.broadcast_to(tile_index + tile_step[None, None, :], full_shape)
    inside = (near_level >= 0) & (near_level < LEVELS) & (near_tile >= 0) & (near_tile < H_TILES)
    centre = (level_step == 0) & (tile_step == 0)
    random_bits = jax.random.randint(key, full_shape, 0, 1 << 20)
    scores = random_bits * 64 + candidate[None, None, :]
    scores = jnp.where(inside, scores, -1 - candidate[None, None, :])
    scores = jnp.where(centre[None, None, :], 1 << 28, scores)
    unused, chosen = lax.top_k(scores, SLOTS)
    pick_level = jnp.take_along_axis(near_level, chosen, axis=2)
    pick_tile = jnp.take_along_axis(near_tile, chosen, axis=2)
    return (pick_level * H_TILES + pick_tile).astype(jnp.int32)


def draw_implicit_columns(key, part):
    key_diag = jax.random.fold_in(key, 11)
    key_off = jax.random.fold_in(key, 23)
    identity = jnp.eye(LEVELS, dtype=jnp.float32)
    diagonal = jax.random.uniform(key_diag, (H_CELLS, LEVELS, 1), jnp.float32, 0.6, 1.0)
    limit = 1.5 / LEVELS ** 0.5
    spread = jax.random.normal(key_off, (H_CELLS, LEVELS, LEVELS), jnp.float32) * (0.3 / LEVELS ** 0.5)
    spread = jnp.clip(spread, -limit, limit)
    return identity * diagonal + (1.0 - identity) * spread


def set_ends(array, rng, least, high):
    longest = array.shape.index(max(array.shape))
    spots = []
    for shift in (0, 1):
        where = [jax.random.randint(jax.random.fold_in(rng, axis), (), 0, length) for axis, length in enumerate(array.shape)]
        where[longest] = (where[longest] + shift) % array.shape[longest]
        spots.append(tuple(where))
    return array.at[spots[0]].set(least).at[spots[1]].set(high)


def shard_levels(stream_key, extent, shards, low, high):
    def one(dim, parts):
        heights = jax.random.uniform(jax.random.fold_in(jax.random.fold_in(stream_key, 6), dim), (parts,), jnp.float32, low / len(shards), high / len(shards))
        return jnp.repeat(jnp.exp(heights), extent[dim] // parts).reshape((-1,) + (1,) * (len(extent) - dim - 1))

    loudness = one(*shards[0])
    for cut in shards[1:]:
        loudness = loudness * one(*cut)
    return loudness


def gaussian(own_key, shape, deviation, most, split=(), kind=jnp.bfloat16):
    factor_of = shard_levels(own_key, shape, split, -0.22, 0.18) if split else 1.0
    entries = jax.random.normal(own_key, shape, jnp.float32) * deviation * factor_of
    return jnp.minimum(jnp.maximum(entries, -most), most).astype(kind)


def setup_inputs(seed: int = 0) -> dict:
    key_list = jax.random.split(jax.random.key(seed), 9)
    tracer = gaussian(key_list[0], (LEVELS, H_CELLS, CLASSES), 1.0, 6.0, ((0, 4), (1, 8)))
    explicit_tiles = gaussian(key_list[1], (LEVELS, H_TILES, SLOTS, TILE, TILE), (TILE * 5) ** -0.5, 0.25, ((0, 4), (1, 8)))
    tile_columns = draw_tile_columns(jax.random.fold_in(key_list[8], 71), 0)
    tile_counts = set_ends(jax.random.randint(key_list[3], (LEVELS, H_TILES), 4, 8), jax.random.fold_in(key_list[3], 1), 4, 7).astype(jnp.int32)
    surface_source = gaussian(key_list[4], (H_CELLS, CLASSES), 1.0, 6.0, ((0, 8),))
    implicit_columns = draw_implicit_columns(jax.random.fold_in(key_list[8], 71), 0)
    settling = jnp.clip(jnp.exp(jax.random.uniform(key_list[6], (CLASSES,), jnp.float32, math.log(0.02), math.log(0.5))), 0.02, 0.5)
    wet_mask = set_ends((jax.random.randint(key_list[7], (LEVELS, H_CELLS), 0, 8) < 7).astype(jnp.int32), jax.random.fold_in(key_list[7], 1), 0, 1)
    return dict(tracer=tracer, explicit_tiles=explicit_tiles, tile_columns=tile_columns, tile_counts=tile_counts, surface_source=surface_source, implicit_columns=implicit_columns, settling=settling, wet_mask=wet_mask)


def reference(tracer, explicit_tiles, tile_columns, tile_counts, surface_source, implicit_columns, settling, wet_mask):
    levels, cell_count, classes = tracer.shape
    tile_size = explicit_tiles.shape[-1]
    h_tiles = cell_count // tile_size
    slot_count = explicit_tiles.shape[2]
    live_slots = (jnp.arange(slot_count, dtype=jnp.int32)[None, None, :] < tile_counts[:, :, None]).astype(jnp.float32)
    fall_rate = settling[None, None, :]
    wet_cells = wet_mask.astype(jnp.float32)[:, :, None]
    current = tracer
    for step_index in range(STEPS):
        all_blocks = current.reshape(levels * h_tiles, tile_size, classes)

        def level_rows(inputs):
            tiles_here, columns_here, live_here = inputs
            picked = all_blocks[columns_here].astype(jnp.float32) * live_here[:, :, None, None]
            return jnp.einsum("tjab,tjbs->tas", tiles_here.astype(jnp.float32), picked)

        explicit_flow = lax.map(level_rows, (explicit_tiles, tile_columns, live_slots))
        explicit_flow = explicit_flow.reshape(levels, cell_count, classes)
        explicit_flow = explicit_flow.at[0].add(surface_source.astype(jnp.float32))
        loaded = explicit_flow.astype(jnp.bfloat16)
        mixed_col = jnp.einsum("ckm,mcs->kcs", implicit_columns, loaded.astype(jnp.float32), precision=lax.Precision.HIGHEST)
        from_above = jnp.concatenate([jnp.zeros_like(mixed_col[:1]), mixed_col[:-1]], axis=0)
        settled = (1.0 - fall_rate) * mixed_col + fall_rate * from_above
        current = (wet_cells * settled).astype(jnp.bfloat16)
    return current
```

```python
import functools

import jax
import jax.numpy as jnp
from jax import lax
from jax.experimental import pallas as pl
from jax.experimental.pallas import tpu as pltpu
from jax.sharding import PartitionSpec as P

REACH = 2
STEPS = 4
Q = 4
MESH = pl.DeviceIdType.MESH
F32 = jnp.float32
BF16 = jnp.bfloat16


def kernel(
    h_size,
    v_size,
    tracer,
    tiles,
    source,
    extra,
    settling,
    columns,
    counts,
    out,
    weights,
    turned,
    gath,
    other,
    final,
    src_t,
    fall,
    ops,
    a_win,
    w_win,
    cols_v,
    cols_s,
    pos,
    send_sem,
    recv_sem,
    first_send,
    first_recv,
    last_send,
    last_recv,
    ops_send,
    ops_recv,
    pair_send,
    pair_recv,
    local_sem,
    *halos,
):
    lev_dev, cells_dev, classes = tracer.shape
    slots, size = tiles.shape[2], tiles.shape[3]
    tiles_dev = cells_dev // size
    window = lev_dev + 2 * REACH
    levels = lev_dev * v_size
    lev_chip = 2 * lev_dev
    h_tiles = h_size * tiles_dev
    half = classes // 2
    ch = half // Q
    blk = tiles_dev * window
    h = lax.axis_index("horiz")
    v = lax.axis_index("vert")
    even = lax.rem(h, 2) == 0
    core = lax.rem(v, 2)
    chip = v // 2
    base = 2 * chip
    part = lax.rem(core + chip + h // 2 + lax.rem(h, 2), 2)
    partner = jnp.where(even, h + 1, h - 1)
    ahead = jnp.where(even, h + 2, h - 2)
    behind = jnp.where(even, h - 2, h + 2)
    has_ahead = (ahead >= 0) & (ahead < h_size)
    has_behind = (behind >= 0) & (behind < h_size)

    def vert(d):
        flipped = v
        if d & 1:
            flipped = flipped + 1 - 2 * core
        if d & 2:
            flipped = lax.rem(flipped + 2, 4)
        return {"horiz": h, "vert": flipped}

    crossed = v + 1 - 2 * core
    near = {"horiz": partner, "vert": crossed}
    front = {"horiz": ahead, "vert": crossed}
    back = {"horiz": behind, "vert": crossed}

    barrier = pltpu.get_barrier_semaphore()
    for where in (vert(1), vert(2), vert(3), near):
        pl.semaphore_signal(barrier, inc=1, device_id=where, device_id_type=MESH)

    @pl.when(has_ahead)
    def _():
        pl.semaphore_signal(barrier, inc=1, device_id=front, device_id_type=MESH)

    @pl.when(has_behind)
    def _():
        pl.semaphore_signal(barrier, inc=1, device_id=back, device_id_type=MESH)

    near_at = jnp.where(even, 2 * blk, 0)
    far_at = jnp.where(even, 0, 2 * blk)

    def copy_to(src, dst, send, recv, where):
        return pltpu.make_async_remote_copy(
            src_ref=src,
            dst_ref=dst,
            send_sem=send,
            recv_sem=recv,
            device_id=where,
            device_id_type=MESH,
        )

    def remote(src, dst, p, q, kind, where):
        return copy_to(
            src, dst, send_sem.at[p, q, kind], recv_sem.at[p, q, kind], where
        )

    def x_copies(p, q):
        if p == 0:
            here = gath.at[0, q, pl.ds(lev_dev * v, lev_dev)]
            return [
                copy_to(
                    here if d == 3 else other.at[q],
                    here,
                    first_send.at[q, d - 1],
                    first_recv.at[q, d - 1],
                    vert(d),
                )
                for d in (3, 2, 1)
            ]
        here = gath.at[p % 2, q, pl.ds(lev_chip * chip, lev_chip)]
        return [remote(here, here, p, q, 0, vert(3))]

    def block(p, q, at):
        return halos[p % 2 * Q + q].at[pl.ds(at, blk)]

    def near_copy(p, q):
        return remote(block(p, q, blk), block(p, q, far_at), p, q, 1, near)

    def front_copy(p, q):
        return remote(block(p, q, near_at), block(p, q, far_at), p, q, 2, front)

    def last_copies(q):
        theirs = lev_dev * (v + 1 - 2 * core) - base
        halo = halos[STEPS % 2 * Q + q]
        return [
            copy_to(
                halo.at[pl.ds(blk + t * window + theirs, lev_dev)],
                final.at[part * Q + q, t],
                last_send.at[q, t],
                last_recv.at[q, t],
                vert(1),
            )
            for t in range(tiles_dev)
        ]

    def pair_copies():
        mine = weights.at[pl.ds(lev_dev * core, lev_dev)]
        cols = cols_v.at[core]
        return [
            copy_to(cols, cols, pair_send.at[0], pair_recv.at[0], vert(1)),
            copy_to(mine, mine, pair_send.at[1], pair_recv.at[1], vert(1)),
        ]

    def load_first(q):
        for level in range(lev_dev):
            for t in range(tiles_dev):
                ours = pl.ds(pl.multiple_of(part * half + q * ch, ch), ch)
                theirs = pl.ds(pl.multiple_of((1 - part) * half + q * ch, ch), ch)
                gath[0, q, lev_dev * v + level, t] = turned[level, t, ours, :]
                other[q, level, t] = turned[level, t, theirs, :]

    def explicit(p, q):
        for level in range(lev_chip):
            for t in range(tiles_dev):
                picked = jnp.concatenate(
                    [
                        halos[(p - 1) % 2 * Q + q][pos[level, t * slots + j]]
                        for j in range(slots)
                    ],
                    axis=1,
                )
                flow = jnp.dot(
                    picked, weights[level, t], preferred_element_type=F32
                )
                if level == 0:
                    ours = pl.ds(pl.multiple_of(part * half + q * ch, ch), ch)
                    flow = flow + src_t[t, ours, :]
                gath[p % 2, q, lev_chip * chip + level, t] = flow.astype(BF16)

    def stage_a(p, q):
        if p == 0:
            load_first(q)
        else:
            explicit(p, q)
        for copy in x_copies(p, q):
            copy.start()

    def sends_done(p, q):
        for copy in x_copies(p, q):
            copy.wait_send()
        if p == STEPS:
            return
        near_copy(p, q).wait_send()

        @pl.when(has_ahead)
        def _():
            front_copy(p, q).wait_send()

    def solve(p, q):
        par = p % 2
        halo = halos[par * Q + q]
        if p == 0:
            for t in range(tiles_dev):
                for k in range(window):
                    halo[blk + t * window + k] = gath[par, q, base + k, t]
            return
        rows = 16

        for t in range(tiles_dev):
            for i in range(ch // rows):
                at = slice(i * rows, (i + 1) * rows)
                loaded = [gath[par, q, m, t, at, :].astype(F32) for m in range(levels)]
                start = part * half + q * ch + i * rows
                rate = fall[pl.ds(pl.multiple_of(start, rows), rows), :]
                stay = 1.0 - rate
                above = None
                for k in range(window + 1):
                    mixed = None
                    for m in range(levels):
                        r = k * levels + m
                        term = a_win[t, r : r + 1, :] * loaded[m]
                        mixed = term if m == 0 else mixed + term
                    if k:
                        settled = stay * mixed + rate * above
                        wet = w_win[t, k - 1 : k, :]
                        halo[blk + t * window + k - 1, at, :] = (wet * settled).astype(BF16)
                    above = mixed

    def stage_b(p, q):
        for copy in x_copies(p, q):
            copy.wait_recv()
        if p:
            sends_done(p - 1, q)
        solve(p, q)
        if p < STEPS:
            near_copy(p, q).start()
        else:
            for copy in last_copies(q):
                copy.start()

    def stage_c(p, q):
        near_copy(p, q).wait_recv()

        @pl.when(has_ahead)
        def _():
            front_copy(p, q).start()

    def stage_d(p, q):
        @pl.when(has_behind)
        def _():
            front_copy(p, q).wait_recv()

    def ops_copy(d):
        return copy_to(
            extra, ops.at[v], ops_send.at[d - 1], ops_recv.at[d - 1], vert(d)
        )

    def prepare():
        for level in range(lev_dev):
            for t in range(tiles_dev):
                for j in range(slots):
                    live = (j < counts[level, t]).astype(F32)
                    weights[lev_dev * core + level, t, j * size : (j + 1) * size, :] = (
                        tiles[level, t, j].astype(F32).T * live
                    ).astype(BF16)

    def prepare_more():
        on_top = (chip == 0).astype(F32)
        for t in range(tiles_dev):
            src_t[t] = source[t * size : (t + 1) * size, :].astype(F32).T * on_top
        fall[...] = jnp.broadcast_to(settling[...], (size, classes)).T

    def positions():
        local = pltpu.make_async_copy(cols_v, cols_s, local_sem)
        local.start()
        local.wait()
        last = 3 * blk - 1
        for level in range(lev_chip):
            for n in range(tiles_dev * slots):
                column = cols_s[level // lev_dev, level % lev_dev, n]
                row = lax.div(column, h_tiles) - base
                across = lax.rem(column, h_tiles) - tiles_dev * h + REACH
                pos[level, n] = jnp.clip(across * window + row, 0, last)

    def operators():
        square = levels * levels
        for t in range(tiles_dev):
            for k in range(window + 1):
                level = base + k - 1
                row = pl.ds(
                    pl.multiple_of(jnp.maximum(level, 0) * levels, levels), levels
                )
                keep = (level >= 0).astype(F32)
                a_win[t, k * levels : (k + 1) * levels, :] = keep * (
                    ops[2 * t, row, :] + ops[2 * t + 1, row, :]
                )
                if k:
                    w_win[t, k - 1 : k, :] = ops[
                        level // lev_dev,
                        pl.ds(square + lax.rem(level, lev_dev) * tiles_dev + t, 1),
                        :,
                    ]

    ops[v] = extra[...]
    cols_v[core] = columns[...]
    for level in range(lev_dev):
        for t in range(tiles_dev):
            turned[level, t] = tracer[level, t * size : (t + 1) * size, :].T
    count = 4 + has_ahead.astype(jnp.int32) + has_behind.astype(jnp.int32)
    pl.semaphore_wait(barrier, count)
    for q in range(Q):
        stage_a(0, q)
    for d in (1, 2, 3):
        ops_copy(d).start()
    pair = pair_copies()
    pair[0].start()
    prepare()
    pair[1].start()
    for q in range(Q):
        stage_b(0, q)
    prepare_more()
    for d in (1, 2, 3):
        ops_copy(d).wait()
    operators()
    pair[0].wait()
    positions()
    for p in range(STEPS):
        for q in range(Q):
            stage_c(p, q)
        if p == 0:
            pair[1].wait()
        for q in range(Q):
            stage_d(p, q)
            stage_a(p + 1, q)
        for q in range(Q):
            stage_b(p + 1, q)
    mine = lev_dev * v - base
    for q in range(Q):
        for t in range(tiles_dev):
            for level in range(lev_dev):
                final[part * Q + q, t, level] = halos[STEPS % 2 * Q + q][
                    blk + t * window + mine + level
                ]
    for q in range(Q):
        for copy in last_copies(q):
            copy.wait_recv()
    for level in range(lev_dev):
        for t in range(tiles_dev):
            whole = jnp.concatenate(
                [final[i, t, level] for i in range(2 * Q)], axis=0
            )
            out[level, t * size : (t + 1) * size, :] = whole.T
    for q in range(Q):
        sends_done(STEPS, q)
        for copy in last_copies(q):
            copy.wait_send()


def on_device(h_size, v_size, tracer, tiles, columns, counts, source, implicit, settling, wet):
    lev_dev, cells_dev, classes = tracer.shape
    slots, size = tiles.shape[2], tiles.shape[3]
    tiles_dev = cells_dev // size
    levels = implicit.shape[1]
    share = implicit.shape[0]
    window = lev_dev + 2 * REACH
    assert lev_dev == 2 and tiles_dev == 2 and v_size == 4 and h_size % 2 == 0
    ch = classes // 2 // Q
    flat = implicit.reshape(share, levels * levels).T
    right = lax.rem(lax.axis_index("vert"), 2).astype(F32)
    flat = jnp.concatenate([flat * (1.0 - right), flat * right], axis=1)
    wet_rows = wet.astype(F32).reshape(lev_dev * tiles_dev, size)
    extra = jnp.concatenate([flat, wet_rows, jnp.zeros_like(wet_rows)], axis=0)
    vm = pl.BlockSpec(memory_space=pltpu.VMEM)
    sm = pl.BlockSpec(memory_space=pltpu.SMEM)
    phases = STEPS + 1
    cols = columns.reshape(lev_dev, tiles_dev * slots)
    cols = jnp.pad(cols, ((0, 8 - lev_dev), (0, 128 - cols.shape[1])))
    dma = pltpu.SemaphoreType.DMA
    return pl.pallas_call(
        functools.partial(kernel, h_size, v_size),
        out_shape=jax.ShapeDtypeStruct(tracer.shape, tracer.dtype),
        in_specs=[vm] * 6 + [sm],
        out_specs=vm,
        scratch_shapes=[
            pltpu.VMEM((2 * lev_dev, tiles_dev, slots * size, size), BF16),
            pltpu.VMEM((lev_dev, tiles_dev, classes, size), BF16),
            pltpu.VMEM((2, Q, levels, tiles_dev, ch, size), BF16),
            pltpu.VMEM((Q, lev_dev, tiles_dev, ch, size), BF16),
            pltpu.VMEM((2 * Q, tiles_dev, lev_dev, ch, size), BF16),
            pltpu.VMEM((tiles_dev, classes, size), F32),
            pltpu.VMEM((classes, size), F32),
            pltpu.VMEM((v_size,) + extra.shape, F32),
            pltpu.VMEM((tiles_dev, (window + 1) * levels, size), F32),
            pltpu.VMEM((tiles_dev, 8, size), F32),
            pltpu.VMEM((2,) + cols.shape, jnp.int32),
            pltpu.SMEM((2,) + cols.shape, jnp.int32),
            pltpu.SMEM((2 * lev_dev, tiles_dev * slots), jnp.int32),
            dma((phases, Q, 3)),
            dma((phases, Q, 3)),
            dma((Q, 3)),
            dma((Q, 3)),
            dma((Q, tiles_dev)),
            dma((Q, tiles_dev)),
            dma((3,)),
            dma((3,)),
            dma((2,)),
            dma((2,)),
            dma(()),
        ]
        + [pltpu.VMEM((3 * tiles_dev * window, ch, size), BF16)] * (2 * Q),
        compiler_params=pltpu.CompilerParams(
            collective_id=0, has_side_effects=True, vmem_limit_bytes=32 * 2**20
        ),
    )(tracer, tiles, source, extra, settling.reshape(1, classes), cols, counts)


def solution(mesh):
    placed = (
        P("vert", "horiz", None),
        P("vert", "horiz", None, None, None),
        P("vert", "horiz", None),
        P("vert", "horiz"),
        P("horiz", None),
        P(("horiz", "vert"), None, None),
        P(),
        P("vert", "horiz"),
    )
    body = functools.partial(on_device, mesh.shape["horiz"], mesh.shape["vert"])
    return jax.shard_map(
        body, mesh=mesh, in_specs=placed, out_specs=P("vert", "horiz", None), check_vma=False
    )
```

```python
import functools

import jax
import jax.numpy as jnp
from jax import lax
from jax.experimental import pallas as pl
from jax.experimental.pallas import tpu as pltpu
from jax.sharding import PartitionSpec as P

REACH = 2
STEPS = 4
Q = 4
ORDER = [
    (late, p, q)
    for when, late, p, q in sorted(
        (6.8 * p + 3.0 * late + 1.05 * q, late, p, q)
        for p in range(1, STEPS + 1)
        for late in range(2)
        for q in range(Q)
        if p + late <= STEPS
    )
]
MESH = pl.DeviceIdType.MESH
ALL = ((1, 1, 1), (1, 1, 0), (1, 0, 0), (1, 0, 1), (0, 1, 1), (0, 1, 0), (0, 0, 1))
SAME = ((1, 1, 1), (1, 0, 0), (0, 1, 1))
F32 = jnp.float32
BF16 = jnp.bfloat16


def kernel(
    h_size,
    v_size,
    tracer,
    tiles,
    source,
    extra,
    settling,
    columns,
    counts,
    out,
    weights,
    turned,
    gath,
    other,
    final,
    src_t,
    fall,
    ops,
    a_win,
    w_win,
    cols_v,
    cols_s,
    pos,
    send_sem,
    recv_sem,
    first_send,
    first_recv,
    last_send,
    last_recv,
    ops_send,
    ops_recv,
    pair_send,
    pair_recv,
    local_sem,
    *halos,
):
    lev_dev, cells_dev, classes = tracer.shape
    slots, size = tiles.shape[2], tiles.shape[3]
    tiles_dev = cells_dev // size
    window = lev_dev + 2 * REACH
    levels = lev_dev * v_size
    lev_chip = 2 * lev_dev
    h_tiles = h_size * tiles_dev
    half = classes // 2
    ch = half // Q
    blk = tiles_dev * window
    h = lax.axis_index("horiz")
    v = lax.axis_index("vert")
    even = lax.rem(h, 2) == 0
    core = lax.rem(v, 2)
    chip = v // 2
    base = 2 * chip
    partner = jnp.where(even, h + 1, h - 1)
    ahead = jnp.where(even, h + 2, h - 2)
    behind = jnp.where(even, h - 2, h + 2)
    has_ahead = (ahead >= 0) & (ahead < h_size)
    has_behind = (behind >= 0) & (behind < h_size)
    part = lax.rem(core + chip + h // 2, 2)
    central = lax.rem(core + chip, 2) == 1

    def target(dy, dx, dc):
        flipped = v
        if dc:
            flipped = flipped + 1 - 2 * core
        if dx:
            flipped = lax.rem(flipped + 2, 4)
        return {"horiz": partner if dy else h, "vert": flipped}

    def vert(d):
        return target(0, d // 2, d % 2)

    crossed = v + 1 - 2 * core
    front = {"horiz": ahead, "vert": crossed}
    back = {"horiz": behind, "vert": crossed}

    barrier = pltpu.get_barrier_semaphore()
    for dy, dx, dc in ALL:
        pl.semaphore_signal(
            barrier, inc=1, device_id=target(dy, dx, dc), device_id_type=MESH
        )

    @pl.when(has_ahead)
    def _():
        pl.semaphore_signal(barrier, inc=1, device_id=front, device_id_type=MESH)

    @pl.when(has_behind)
    def _():
        pl.semaphore_signal(barrier, inc=1, device_id=back, device_id_type=MESH)

    near_at = jnp.where(even, 2 * blk, 0)
    far_at = jnp.where(even, 0, 2 * blk)

    def copy_to(src, dst, send, recv, where):
        return pltpu.make_async_remote_copy(
            src_ref=src,
            dst_ref=dst,
            send_sem=send,
            recv_sem=recv,
            device_id=where,
            device_id_type=MESH,
        )

    def remote(src, dst, p, q, kind, where):
        return copy_to(
            src, dst, send_sem.at[p, q, kind], recv_sem.at[p, q, kind], where
        )

    def first_copy(q, n):
        dy, dx, dc = ALL[n]
        mine = gath.at[0, q, 0, pl.ds(lev_dev * v, lev_dev)]
        return copy_to(
            other.at[q] if (dx + dc) % 2 else mine,
            gath.at[0, q, dy, pl.ds(lev_dev * v, lev_dev)],
            first_send.at[q, n],
            first_recv.at[q, n],
            target(dy, dx, dc),
        )

    def first_all(q, sending, act):
        for n, (dy, dx, dc) in enumerate(ALL):
            if not dx:
                act(first_copy(q, n))
                continue
            wanted = central if sending or dc else ~central

            @pl.when(wanted)
            def _():
                act(first_copy(q, n))

    def step_copy(p, q, n):
        dy, dx, dc = SAME[n]
        mine = gath.at[p % 2, q, 0, pl.ds(lev_chip * chip, lev_chip)]
        theirs = gath.at[p % 2, q, dy, pl.ds(lev_chip * chip, lev_chip)]
        return remote(mine, theirs, p, q, n, target(dy, dx, dc))

    def step_copies(p, q):
        kinds = (2,) if p == STEPS else (0, 1, 2)
        return [step_copy(p, q, n) for n in kinds]

    def block(p, q, at):
        return halos[p % 2 * Q + q].at[pl.ds(at, blk)]

    def front_copy(p, q):
        return remote(block(p, q, near_at), block(p, q, far_at), p, q, 3, front)

    def last_copies(q):
        theirs = lev_dev * (v + 1 - 2 * core) - base
        halo = halos[STEPS % 2 * Q + q]
        return [
            copy_to(
                halo.at[pl.ds(blk + t * window + theirs, lev_dev)],
                final.at[part * Q + q, t],
                last_send.at[q, t],
                last_recv.at[q, t],
                vert(1),
            )
            for t in range(tiles_dev)
        ]

    def pair_copies():
        mine = weights.at[pl.ds(lev_dev * core, lev_dev)]
        cols = cols_v.at[core]
        return [
            copy_to(cols, cols, pair_send.at[0], pair_recv.at[0], vert(1)),
            copy_to(mine, mine, pair_send.at[1], pair_recv.at[1], vert(1)),
        ]

    def load_first(q):
        for level in range(lev_dev):
            for t in range(tiles_dev):
                ours = pl.ds(pl.multiple_of(part * half + q * ch, ch), ch)
                theirs = pl.ds(pl.multiple_of((1 - part) * half + q * ch, ch), ch)
                gath[0, q, 0, lev_dev * v + level, t] = turned[level, t, ours, :]
                other[q, level, t] = turned[level, t, theirs, :]

    def explicit(p, q):
        for level in range(lev_chip):
            for t in range(tiles_dev):
                picked = jnp.concatenate(
                    [
                        halos[(p - 1) % 2 * Q + q][pos[level, t * slots + j]]
                        for j in range(slots)
                    ],
                    axis=1,
                )
                flow = jnp.dot(
                    picked, weights[level, t], preferred_element_type=F32
                )
                if level == 0:
                    ours = pl.ds(pl.multiple_of(part * half + q * ch, ch), ch)
                    flow = flow + src_t[t, ours, :]
                gath[p % 2, q, 0, lev_chip * chip + level, t] = flow.astype(BF16)

    def stage_a(p, q):
        if p == 0:
            load_first(q)
            first_all(q, True, lambda copy: copy.start())
            return
        if p == 1:
            first_all(q, True, lambda copy: copy.wait_send())
        else:
            for copy in step_copies(p - 1, q):
                copy.wait_send()

        @pl.when(has_behind)
        def _():
            front_copy(p - 1, q).wait_recv()

        explicit(p, q)
        for copy in step_copies(p, q):
            copy.start()

    def solve(p, q, which):
        par = p % 2
        halo = halos[par * Q + q]
        at0 = near_at if which else blk
        if p == 0:
            for t in range(tiles_dev):
                for k in range(window):
                    halo[at0 + t * window + k] = gath[par, q, which, base + k, t]
            return
        rows = 16

        for t in range(tiles_dev):
            for i in range(ch // rows):
                at = slice(i * rows, (i + 1) * rows)
                loaded = [
                    gath[par, q, which, m, t, at, :].astype(F32) for m in range(levels)
                ]
                start = part * half + q * ch + i * rows
                rate = fall[pl.ds(pl.multiple_of(start, rows), rows), :]
                stay = 1.0 - rate
                above = None
                for k in range(window + 1):
                    mixed = None
                    for m in range(levels):
                        r = k * levels + m
                        term = a_win[which, t, r : r + 1, :] * loaded[m]
                        mixed = term if m == 0 else mixed + term
                    if k:
                        settled = stay * mixed + rate * above
                        wet = w_win[which, t, k - 1 : k, :]
                        halo[at0 + t * window + k - 1, at, :] = (wet * settled).astype(
                            BF16
                        )
                    above = mixed

    def stage_b(p, q):
        if p == 0:
            first_all(q, False, lambda copy: copy.wait_recv())
        elif p < STEPS:
            step_copy(p, q, 0).wait_recv()
            step_copy(p, q, 1).wait_recv()
        if p:

            @pl.when(has_ahead)
            def _():
                front_copy(p - 1, q).wait_send()

        if p < STEPS:
            solve(p, q, 1)

            @pl.when(has_ahead)
            def _():
                front_copy(p, q).start()

        if p:
            step_copy(p, q, 2).wait_recv()
        solve(p, q, 0)
        if p == STEPS:
            for copy in last_copies(q):
                copy.start()

    def ops_copy(n):
        dy, dx, dc = ALL[n]
        return copy_to(
            extra, ops.at[dy, v], ops_send.at[n], ops_recv.at[n], target(dy, dx, dc)
        )

    def prepare():
        for level in range(lev_dev):
            for t in range(tiles_dev):
                for j in range(slots):
                    live = (j < counts[level, t]).astype(F32)
                    weights[lev_dev * core + level, t, j * size : (j + 1) * size, :] = (
                        tiles[level, t, j].astype(F32).T * live
                    ).astype(BF16)

    def prepare_more():
        on_top = (chip == 0).astype(F32)
        for t in range(tiles_dev):
            src_t[t] = source[t * size : (t + 1) * size, :].astype(F32).T * on_top
        fall[...] = jnp.broadcast_to(settling[...], (size, classes)).T

    def positions():
        local = pltpu.make_async_copy(cols_v, cols_s, local_sem)
        local.start()
        local.wait()
        last = 3 * blk - 1
        for level in range(lev_chip):
            for n in range(tiles_dev * slots):
                column = cols_s[level // lev_dev, level % lev_dev, n]
                row = lax.div(column, h_tiles) - base
                across = lax.rem(column, h_tiles) - tiles_dev * h + REACH
                pos[level, n] = jnp.clip(across * window + row, 0, last)

    def operators():
        square = levels * levels
        for which in range(2):
            for t in range(tiles_dev):
                for k in range(window + 1):
                    level = base + k - 1
                    row = pl.ds(
                        pl.multiple_of(jnp.maximum(level, 0) * levels, levels), levels
                    )
                    keep = (level >= 0).astype(F32)
                    a_win[which, t, k * levels : (k + 1) * levels, :] = keep * (
                        ops[which, 2 * t, row, :] + ops[which, 2 * t + 1, row, :]
                    )
                    if k:
                        w_win[which, t, k - 1 : k, :] = ops[
                            which,
                            level // lev_dev,
                            pl.ds(square + lax.rem(level, lev_dev) * tiles_dev + t, 1),
                            :,
                        ]

    ops[0, v] = extra[...]
    cols_v[core] = columns[...]
    for level in range(lev_dev):
        for t in range(tiles_dev):
            turned[level, t] = tracer[level, t * size : (t + 1) * size, :].T
    count = len(ALL) + has_ahead.astype(jnp.int32) + has_behind.astype(jnp.int32)
    pl.semaphore_wait(barrier, count)
    for q in range(Q):
        stage_a(0, q)
    pair = pair_copies()
    pair[0].start()
    for n in range(len(ALL)):
        ops_copy(n).start()
    prepare()
    pair[1].start()
    for q in range(Q):
        stage_b(0, q)
    prepare_more()
    pair[0].wait()
    positions()
    pair[1].wait()
    for q in range(Q):
        stage_a(1, q)
    for n in range(len(ALL)):
        ops_copy(n).wait()
    operators()
    for late, p, q in ORDER:
        if late:
            stage_a(p + 1, q)
        else:
            stage_b(p, q)
    mine = lev_dev * v - base
    for q in range(Q):
        for t in range(tiles_dev):
            for level in range(lev_dev):
                final[part * Q + q, t, level] = halos[STEPS % 2 * Q + q][
                    blk + t * window + mine + level
                ]
    for q in range(Q):
        for copy in last_copies(q):
            copy.wait_recv()
    for level in range(lev_dev):
        for t in range(tiles_dev):
            whole = jnp.concatenate(
                [final[i, t, level] for i in range(2 * Q)], axis=0
            )
            out[level, t * size : (t + 1) * size, :] = whole.T
    for q in range(Q):
        for copy in step_copies(STEPS, q) + last_copies(q):
            copy.wait_send()


def on_device(h_size, v_size, tracer, tiles, columns, counts, source, implicit, settling, wet):
    lev_dev, cells_dev, classes = tracer.shape
    slots, size = tiles.shape[2], tiles.shape[3]
    tiles_dev = cells_dev // size
    levels = implicit.shape[1]
    share = implicit.shape[0]
    window = lev_dev + 2 * REACH
    assert lev_dev == 2 and tiles_dev == 2 and v_size == 4 and h_size % 2 == 0
    ch = classes // 2 // Q
    flat = implicit.reshape(share, levels * levels).T
    right = lax.rem(lax.axis_index("vert"), 2).astype(F32)
    flat = jnp.concatenate([flat * (1.0 - right), flat * right], axis=1)
    wet_rows = wet.astype(F32).reshape(lev_dev * tiles_dev, size)
    extra = jnp.concatenate([flat, wet_rows, jnp.zeros_like(wet_rows)], axis=0)
    vm = pl.BlockSpec(memory_space=pltpu.VMEM)
    sm = pl.BlockSpec(memory_space=pltpu.SMEM)
    phases = STEPS + 1
    cols = columns.reshape(lev_dev, tiles_dev * slots)
    cols = jnp.pad(cols, ((0, 8 - lev_dev), (0, 128 - cols.shape[1])))
    dma = pltpu.SemaphoreType.DMA
    return pl.pallas_call(
        functools.partial(kernel, h_size, v_size),
        out_shape=jax.ShapeDtypeStruct(tracer.shape, tracer.dtype),
        in_specs=[vm] * 6 + [sm],
        out_specs=vm,
        scratch_shapes=[
            pltpu.VMEM((2 * lev_dev, tiles_dev, slots * size, size), BF16),
            pltpu.VMEM((lev_dev, tiles_dev, classes, size), BF16),
            pltpu.VMEM((2, Q, 2, levels, tiles_dev, ch, size), BF16),
            pltpu.VMEM((Q, lev_dev, tiles_dev, ch, size), BF16),
            pltpu.VMEM((2 * Q, tiles_dev, lev_dev, ch, size), BF16),
            pltpu.VMEM((tiles_dev, classes, size), F32),
            pltpu.VMEM((classes, size), F32),
            pltpu.VMEM((2, v_size) + extra.shape, F32),
            pltpu.VMEM((2, tiles_dev, (window + 1) * levels, size), F32),
            pltpu.VMEM((2, tiles_dev, 8, size), F32),
            pltpu.VMEM((2,) + cols.shape, jnp.int32),
            pltpu.SMEM((2,) + cols.shape, jnp.int32),
            pltpu.SMEM((2 * lev_dev, tiles_dev * slots), jnp.int32),
            dma((phases, Q, 4)),
            dma((phases, Q, 4)),
            dma((Q, len(ALL))),
            dma((Q, len(ALL))),
            dma((Q, tiles_dev)),
            dma((Q, tiles_dev)),
            dma((len(ALL),)),
            dma((len(ALL),)),
            dma((2,)),
            dma((2,)),
            dma(()),
        ]
        + [pltpu.VMEM((3 * tiles_dev * window, ch, size), BF16)] * (2 * Q),
        compiler_params=pltpu.CompilerParams(
            collective_id=0, has_side_effects=True, vmem_limit_bytes=32 * 2**20
        ),
    )(tracer, tiles, source, extra, settling.reshape(1, classes), cols, counts)


def solution(mesh):
    placed = (
        P("vert", "horiz", None),
        P("vert", "horiz", None, None, None),
        P("vert", "horiz", None),
        P("vert", "horiz"),
        P("horiz", None),
        P(("horiz", "vert"), None, None),
        P(),
        P("vert", "horiz"),
    )
    body = functools.partial(on_device, mesh.shape["horiz"], mesh.shape["vert"])
    return jax.shard_map(
        body, mesh=mesh, in_specs=placed, out_specs=P("vert", "horiz", None), check_vma=False
    )
```

```python
import functools

import jax
import jax.numpy as jnp
from jax import lax
from jax.experimental import pallas as pl
from jax.experimental.pallas import tpu as pltpu
from jax.sharding import PartitionSpec as P

REACH = 2
STEPS = 4
Q = 4
ORDER = [
    (late, p, q)
    for when, late, p, q in sorted(
        (6.8 * p + 3.0 * late + 1.4 * q, late, p, q)
        for p in range(1, STEPS + 1)
        for late in range(2)
        for q in range(Q)
        if p + late <= STEPS
    )
]
MESH = pl.DeviceIdType.MESH
ALL = ((1, 1, 1), (1, 1, 0), (1, 0, 0), (1, 0, 1), (0, 1, 1), (0, 1, 0), (0, 0, 1))
SAME = ((1, 1, 1), (1, 0, 0), (0, 1, 1))
F32 = jnp.float32
BF16 = jnp.bfloat16


def kernel(
    h_size,
    v_size,
    tracer_hbm,
    tiles_hbm,
    columns_hbm,
    counts_hbm,
    source_hbm,
    flat_hbm,
    settling_hbm,
    wet_hbm,
    out,
    tracer,
    tiles,
    counts,
    source,
    flat,
    settling,
    wet,
    extra,
    weights,
    turned,
    gath,
    other,
    final,
    src_t,
    fall,
    ops,
    a_full,
    a_win,
    w_win,
    cols_v,
    cols_s,
    pos,
    send_sem,
    recv_sem,
    first_send,
    first_recv,
    last_send,
    last_recv,
    ops_send,
    ops_recv,
    pass_send,
    pass_recv,
    pair_send,
    pair_recv,
    local_sem,
    load_sem,
    *halos,
):
    lev_dev, cells_dev, classes = tracer.shape
    slots, size = tiles.shape[2], tiles.shape[3]
    tiles_dev = cells_dev // size
    window = lev_dev + 2 * REACH
    levels = lev_dev * v_size
    lev_chip = 2 * lev_dev
    h_tiles = h_size * tiles_dev
    half = classes // 2
    ch = half // Q
    blk = tiles_dev * window
    h = lax.axis_index("horiz")
    v = lax.axis_index("vert")
    even = lax.rem(h, 2) == 0
    core = lax.rem(v, 2)
    chip = v // 2
    base = 2 * chip
    partner = jnp.where(even, h + 1, h - 1)
    ahead = jnp.where(even, h + 2, h - 2)
    behind = jnp.where(even, h - 2, h + 2)
    has_ahead = (ahead >= 0) & (ahead < h_size)
    has_behind = (behind >= 0) & (behind < h_size)
    part = lax.rem(core + chip + h // 2, 2)
    central = lax.rem(core + chip, 2) == 1

    def target(dy, dx, dc):
        flipped = v
        if dc:
            flipped = flipped + 1 - 2 * core
        if dx:
            flipped = lax.rem(flipped + 2, 4)
        return {"horiz": partner if dy else h, "vert": flipped}

    def vert(d):
        return target(0, d // 2, d % 2)

    loads = [
        pltpu.make_async_copy(src, dst, load_sem.at[n])
        for n, (src, dst) in enumerate(
            (
                (tracer_hbm, tracer),
                (columns_hbm, cols_v.at[core]),
                (flat_hbm, flat),
                (wet_hbm, wet),
                (counts_hbm, counts),
                (settling_hbm, settling),
                (source_hbm, source),
                (tiles_hbm, tiles),
            )
        )
    ]
    for load in loads:
        load.start()

    crossed = v + 1 - 2 * core
    front = {"horiz": ahead, "vert": crossed}
    back = {"horiz": behind, "vert": crossed}

    barrier = pltpu.get_barrier_semaphore()
    for dy, dx, dc in ALL:
        pl.semaphore_signal(
            barrier, inc=1, device_id=target(dy, dx, dc), device_id_type=MESH
        )

    @pl.when(has_ahead)
    def _():
        pl.semaphore_signal(barrier, inc=1, device_id=front, device_id_type=MESH)

    @pl.when(has_behind)
    def _():
        pl.semaphore_signal(barrier, inc=1, device_id=back, device_id_type=MESH)

    near_at = jnp.where(even, 2 * blk, 0)
    far_at = jnp.where(even, 0, 2 * blk)

    def copy_to(src, dst, send, recv, where):
        return pltpu.make_async_remote_copy(
            src_ref=src,
            dst_ref=dst,
            send_sem=send,
            recv_sem=recv,
            device_id=where,
            device_id_type=MESH,
        )

    def remote(src, dst, p, q, kind, where):
        return copy_to(
            src, dst, send_sem.at[p, q, kind], recv_sem.at[p, q, kind], where
        )

    def first_copy(q, n):
        dy, dx, dc = ALL[n]
        mine = gath.at[0, q, 0, pl.ds(lev_dev * v, lev_dev)]
        return copy_to(
            other.at[q] if (dx + dc) % 2 else mine,
            gath.at[0, q, dy, pl.ds(lev_dev * v, lev_dev)],
            first_send.at[q, n],
            first_recv.at[q, n],
            target(dy, dx, dc),
        )

    def first_all(q, sending, act):
        for n, (dy, dx, dc) in enumerate(ALL):
            if not dx:
                act(first_copy(q, n))
                continue
            wanted = central if sending or dc else ~central

            @pl.when(wanted)
            def _():
                act(first_copy(q, n))

    def step_copy(p, q, n):
        dy, dx, dc = SAME[n]
        mine = gath.at[p % 2, q, 0, pl.ds(lev_chip * chip, lev_chip)]
        theirs = gath.at[p % 2, q, dy, pl.ds(lev_chip * chip, lev_chip)]
        return remote(mine, theirs, p, q, n, target(dy, dx, dc))

    def step_copies(p, q):
        kinds = (2,) if p == STEPS else (0, 1, 2)
        return [step_copy(p, q, n) for n in kinds]

    def block(p, q, at):
        return halos[p % 2 * Q + q].at[pl.ds(at, blk)]

    def front_copy(p, q):
        return remote(block(p, q, near_at), block(p, q, far_at), p, q, 3, front)

    def last_copies(q):
        theirs = lev_dev * (v + 1 - 2 * core) - base
        halo = halos[STEPS % 2 * Q + q]
        return [
            copy_to(
                halo.at[pl.ds(blk + t * window + theirs, lev_dev)],
                final.at[part * Q + q, t],
                last_send.at[q, t],
                last_recv.at[q, t],
                vert(1),
            )
            for t in range(tiles_dev)
        ]

    def pair_copies():
        mine = weights.at[pl.ds(lev_dev * core, lev_dev)]
        cols = cols_v.at[core]
        return [
            copy_to(cols, cols, pair_send.at[0], pair_recv.at[0], vert(1)),
            copy_to(mine, mine, pair_send.at[1], pair_recv.at[1], vert(1)),
        ]

    def load_first(q):
        for level in range(lev_dev):
            for t in range(tiles_dev):
                ours = pl.ds(pl.multiple_of(part * half + q * ch, ch), ch)
                theirs = pl.ds(pl.multiple_of((1 - part) * half + q * ch, ch), ch)
                gath[0, q, 0, lev_dev * v + level, t] = turned[level, t, ours, :]
                other[q, level, t] = turned[level, t, theirs, :]

    def explicit(p, q):
        for level in range(lev_chip):
            for t in range(tiles_dev):
                picked = jnp.concatenate(
                    [
                        halos[(p - 1) % 2 * Q + q][pos[level, t * slots + j]]
                        for j in range(slots)
                    ],
                    axis=1,
                )
                flow = jnp.dot(
                    picked, weights[level, t], preferred_element_type=F32
                )
                if level == 0:
                    ours = pl.ds(pl.multiple_of(part * half + q * ch, ch), ch)
                    flow = flow + src_t[t, ours, :]
                gath[p % 2, q, 0, lev_chip * chip + level, t] = flow.astype(BF16)

    def stage_a(p, q):
        if p == 0:
            first_all(q, True, lambda copy: copy.start())
            return
        if p == 1:
            first_all(q, True, lambda copy: copy.wait_send())
        else:
            for copy in step_copies(p - 1, q):
                copy.wait_send()

        @pl.when(has_behind)
        def _():
            front_copy(p - 1, q).wait_recv()

        explicit(p, q)
        for copy in step_copies(p, q):
            copy.start()

    def solve(p, q, which):
        par = p % 2
        halo = halos[par * Q + q]
        at0 = near_at if which else blk
        if p == 0:
            for t in range(tiles_dev):
                for k in range(window):
                    halo[at0 + t * window + k] = gath[par, q, which, base + k, t]
            return
        rows = 16

        for t in range(tiles_dev):
            for i in range(ch // rows):
                at = slice(i * rows, (i + 1) * rows)
                loaded = [
                    gath[par, q, which, m, t, at, :].astype(F32) for m in range(levels)
                ]
                start = part * half + q * ch + i * rows
                rate = fall[pl.ds(pl.multiple_of(start, rows), rows), :]
                stay = 1.0 - rate
                above = None
                for k in range(window + 1):
                    mixed = None
                    for m in range(levels):
                        r = k * levels + m
                        term = a_win[which, t, r : r + 1, :] * loaded[m]
                        mixed = term if m == 0 else mixed + term
                    if k:
                        settled = stay * mixed + rate * above
                        wet = w_win[which, t, k - 1 : k, :]
                        halo[at0 + t * window + k - 1, at, :] = (wet * settled).astype(
                            BF16
                        )
                    above = mixed

    def stage_b(p, q):
        if p == 0:
            first_all(q, False, lambda copy: copy.wait_recv())
        elif p < STEPS:
            step_copy(p, q, 0).wait_recv()
            step_copy(p, q, 1).wait_recv()
        if p:

            @pl.when(has_ahead)
            def _():
                front_copy(p - 1, q).wait_send()

        if p < STEPS:
            solve(p, q, 1)

            @pl.when(has_ahead)
            def _():
                front_copy(p, q).start()

        if p:
            step_copy(p, q, 2).wait_recv()
        solve(p, q, 0)
        if p == STEPS:
            for copy in last_copies(q):
                copy.start()

    def ops_copy(n):
        dy, dx, dc = SAME[n]
        return copy_to(
            extra, ops.at[dy, v], ops_send.at[n], ops_recv.at[n], target(dy, dx, dc)
        )

    def pass_copies():
        across = v_size - 1 - v
        return [
            copy_to(
                ops.at[dy, at],
                ops.at[dy, at],
                pass_send.at[dy, n],
                pass_recv.at[dy, n],
                vert(1),
            )
            for dy in range(2)
            for n, at in enumerate((v, across))
        ]

    def pack():
        rows = levels * levels // 2
        extra[:rows, :] = jnp.concatenate([flat[:rows, :], flat[rows:, :]], axis=1)
        extra[rows:, :] = jnp.zeros((8, size), F32)
        for level in range(lev_dev):
            for t in range(tiles_dev):
                at = rows + level * tiles_dev + t
                extra[at : at + 1, :] = wet[
                    level : level + 1, t * size : (t + 1) * size
                ].astype(F32)
        ops[0, v] = extra[...]

    def prepare():
        for level in range(lev_dev):
            for t in range(tiles_dev):
                for j in range(slots):
                    live = (j < counts[level, t]).astype(F32)
                    weights[lev_dev * core + level, t, j * size : (j + 1) * size, :] = (
                        tiles[level, t, j].astype(F32).T * live
                    ).astype(BF16)

    def prepare_more():
        on_top = (chip == 0).astype(F32)
        for t in range(tiles_dev):
            src_t[t] = source[t * size : (t + 1) * size, :].astype(F32).T * on_top
        fall[...] = jnp.broadcast_to(settling[...], (size, classes)).T

    def positions():
        local = pltpu.make_async_copy(cols_v, cols_s, local_sem)
        local.start()
        local.wait()
        last = 3 * blk - 1
        for level in range(lev_chip):
            for n in range(tiles_dev * slots):
                column = cols_s[
                    level // lev_dev, level % lev_dev, n // slots, n % slots
                ]
                row = lax.div(column, h_tiles) - base
                across = lax.rem(column, h_tiles) - tiles_dev * h + REACH
                pos[level, n] = jnp.clip(across * window + row, 0, last)

    def operators():
        rows = levels * levels // 2
        for which in range(2):
            for t in range(tiles_dev):
                a = ops[which, 2 * t, :rows, :]
                b = ops[which, 2 * t + 1, :rows, :]
                on_left = lax.broadcasted_iota(jnp.int32, a.shape, 1) < size // 2
                a_full[:levels, :] = jnp.zeros((levels, size), F32)
                a_full[levels : levels + rows, :] = jnp.where(
                    on_left, a, pltpu.roll(b, size // 2, 1)
                )
                a_full[levels + rows :, :] = jnp.where(
                    on_left, pltpu.roll(a, size // 2, 1), b
                )
                for k in range(window + 1):
                    level = base + k - 1
                    row = pl.ds(pl.multiple_of((level + 1) * levels, levels), levels)
                    a_win[which, t, k * levels : (k + 1) * levels, :] = a_full[row, :]
                    if k:
                        w_win[which, t, k - 1 : k, :] = ops[
                            which,
                            level // lev_dev,
                            pl.ds(rows + lax.rem(level, lev_dev) * tiles_dev + t, 1),
                            :,
                        ]

    for level in range(lev_dev):
        for t in range(tiles_dev):
            if level == t == 0:
                loads[0].wait()
            turned[level, t] = tracer[level, t * size : (t + 1) * size, :].T
    for q in range(Q):
        load_first(q)
    count = len(ALL) + has_ahead.astype(jnp.int32) + has_behind.astype(jnp.int32)
    pl.semaphore_wait(barrier, count)
    for q in range(Q):
        stage_a(0, q)
    for load in loads[1:-1]:
        load.wait()
    pair = pair_copies()
    pair[0].start()
    pack()
    for n in range(len(SAME)):
        ops_copy(n).start()
    loads[-1].wait()
    prepare()
    pair[1].start()
    for q in range(Q):
        stage_b(0, q)
    for n in range(len(SAME)):
        ops_copy(n).wait()
    for copy in pass_copies():
        copy.start()
    prepare_more()
    pair[0].wait()
    positions()
    pair[1].wait()
    for q in range(Q):
        stage_a(1, q)
    for copy in pass_copies():
        copy.wait()
    operators()
    for late, p, q in ORDER:
        if late:
            stage_a(p + 1, q)
        else:
            stage_b(p, q)
    mine = lev_dev * v - base
    for q in range(Q):
        for t in range(tiles_dev):
            for level in range(lev_dev):
                final[part * Q + q, t, level] = halos[STEPS % 2 * Q + q][
                    blk + t * window + mine + level
                ]
    for q in range(Q):
        for copy in last_copies(q):
            copy.wait_recv()
    for level in range(lev_dev):
        for t in range(tiles_dev):
            whole = jnp.concatenate(
                [final[i, t, level] for i in range(2 * Q)], axis=0
            )
            out[level, t * size : (t + 1) * size, :] = whole.T
    for q in range(Q):
        for copy in step_copies(STEPS, q) + last_copies(q):
            copy.wait_send()


def on_device(h_size, v_size, tracer, tiles, columns, counts, source, implicit, settling, wet):
    lev_dev, cells_dev, classes = tracer.shape
    slots, size = tiles.shape[2], tiles.shape[3]
    tiles_dev = cells_dev // size
    levels = implicit.shape[1]
    share = implicit.shape[0]
    window = lev_dev + 2 * REACH
    assert lev_dev == 2 and tiles_dev == 2 and v_size == 4 and h_size % 2 == 0
    ch = classes // 2 // Q
    flat = implicit.reshape(share, levels * levels).T
    settling = settling.reshape(1, classes)
    extra = (levels * levels // 2 + 8, size)
    hbm = pl.BlockSpec(memory_space=pl.ANY)
    vm = pl.BlockSpec(memory_space=pltpu.VMEM)
    phases = STEPS + 1
    dma = pltpu.SemaphoreType.DMA
    return pl.pallas_call(
        functools.partial(kernel, h_size, v_size),
        out_shape=jax.ShapeDtypeStruct(tracer.shape, tracer.dtype),
        in_specs=[hbm] * 8,
        out_specs=vm,
        scratch_shapes=[
            pltpu.VMEM(tracer.shape, BF16),
            pltpu.VMEM(tiles.shape, BF16),
            pltpu.SMEM(counts.shape, jnp.int32),
            pltpu.VMEM(source.shape, BF16),
            pltpu.VMEM(flat.shape, F32),
            pltpu.VMEM(settling.shape, F32),
            pltpu.VMEM(wet.shape, jnp.int32),
            pltpu.VMEM(extra, F32),
            pltpu.VMEM((2 * lev_dev, tiles_dev, slots * size, size), BF16),
            pltpu.VMEM((lev_dev, tiles_dev, classes, size), BF16),
            pltpu.VMEM((2, Q, 2, levels, tiles_dev, ch, size), BF16),
            pltpu.VMEM((Q, lev_dev, tiles_dev, ch, size), BF16),
            pltpu.VMEM((2 * Q, tiles_dev, lev_dev, ch, size), BF16),
            pltpu.VMEM((tiles_dev, classes, size), F32),
            pltpu.VMEM((classes, size), F32),
            pltpu.VMEM((2, v_size) + extra, F32),
            pltpu.VMEM(((levels + 1) * levels, size), F32),
            pltpu.VMEM((2, tiles_dev, (window + 1) * levels, size), F32),
            pltpu.VMEM((2, tiles_dev, 8, size), F32),
            pltpu.VMEM((2,) + columns.shape, jnp.int32),
            pltpu.SMEM((2,) + columns.shape, jnp.int32),
            pltpu.SMEM((2 * lev_dev, tiles_dev * slots), jnp.int32),
            dma((phases, Q, 4)),
            dma((phases, Q, 4)),
            dma((Q, len(ALL))),
            dma((Q, len(ALL))),
            dma((Q, tiles_dev)),
            dma((Q, tiles_dev)),
            dma((len(SAME),)),
            dma((len(SAME),)),
            dma((2, 2)),
            dma((2, 2)),
            dma((2,)),
            dma((2,)),
            dma(()),
            dma((8,)),
        ]
        + [pltpu.VMEM((3 * tiles_dev * window, ch, size), BF16)] * (2 * Q),
        compiler_params=pltpu.CompilerParams(
            collective_id=0, has_side_effects=True, vmem_limit_bytes=56 * 2**20
        ),
    )(tracer, tiles, columns, counts, source, flat, settling, wet)


def solution(mesh):
    placed = (
        P("vert", "horiz", None),
        P("vert", "horiz", None, None, None),
        P("vert", "horiz", None),
        P("vert", "horiz"),
        P("horiz", None),
        P(("horiz", "vert"), None, None),
        P(),
        P("vert", "horiz"),
    )
    body = functools.partial(on_device, mesh.shape["horiz"], mesh.shape["vert"])
    return jax.shard_map(
        body, mesh=mesh, in_specs=placed, out_specs=P("vert", "horiz", None), check_vma=False
    )
```

```python
import functools

import jax
import jax.numpy as jnp
from jax import lax
from jax.experimental import pallas as pl
from jax.experimental.pallas import tpu as pltpu
from jax.sharding import PartitionSpec as P

REACH = 2
STEPS = 4
Q = 4
ORDER = [
    (late, p, q)
    for when, late, p, q in sorted(
        (6.8 * p + 3.0 * late + 1.4 * q, late, p, q)
        for p in range(1, STEPS + 1)
        for late in range(2)
        for q in range(Q)
        if p + late <= STEPS
    )
]
MESH = pl.DeviceIdType.MESH
ALL = ((1, 1, 1), (1, 1, 0), (1, 0, 0), (1, 0, 1), (0, 1, 1), (0, 1, 0), (0, 0, 1))
SAME = ((1, 1, 1), (1, 0, 0), (0, 1, 1))
F32 = jnp.float32
BF16 = jnp.bfloat16


def kernel(
    h_size,
    v_size,
    tracer_hbm,
    tiles_hbm,
    columns_hbm,
    counts_hbm,
    source_hbm,
    flat_hbm,
    settling_hbm,
    wet_hbm,
    out,
    tracer,
    tiles,
    counts,
    source,
    flat,
    settling,
    wet,
    extra,
    weights,
    turned,
    gath,
    other,
    final,
    src_t,
    fall,
    ops,
    a_full,
    a_win,
    w_win,
    cols_v,
    cols_s,
    pos,
    send_sem,
    recv_sem,
    first_send,
    first_recv,
    last_send,
    last_recv,
    ops_send,
    ops_recv,
    pass_send,
    pass_recv,
    pair_send,
    pair_recv,
    local_sem,
    load_sem,
    *halos,
):
    lev_dev, cells_dev, classes = tracer.shape
    slots, size = tiles.shape[2], tiles.shape[3]
    tiles_dev = cells_dev // size
    window = lev_dev + 2 * REACH
    levels = lev_dev * v_size
    lev_chip = 2 * lev_dev
    h_tiles = h_size * tiles_dev
    half = classes // 2
    ch = half // Q
    blk = tiles_dev * window
    h = lax.axis_index("horiz")
    v = lax.axis_index("vert")
    even = lax.rem(h, 2) == 0
    core = lax.rem(v, 2)
    chip = v // 2
    base = 2 * chip
    partner = jnp.where(even, h + 1, h - 1)
    ahead = jnp.where(even, h + 2, h - 2)
    behind = jnp.where(even, h - 2, h + 2)
    has_ahead = (ahead >= 0) & (ahead < h_size)
    has_behind = (behind >= 0) & (behind < h_size)
    part = lax.rem(core + chip + h // 2, 2)
    central = lax.rem(core + chip, 2) == 1

    def target(dy, dx, dc):
        flipped = v
        if dc:
            flipped = flipped + 1 - 2 * core
        if dx:
            flipped = lax.rem(flipped + 2, 4)
        return {"horiz": partner if dy else h, "vert": flipped}

    def vert(d):
        return target(0, d // 2, d % 2)

    loads = [
        pltpu.make_async_copy(src, dst, load_sem.at[n])
        for n, (src, dst) in enumerate(
            (
                (tracer_hbm, tracer),
                (columns_hbm, cols_v.at[core]),
                (flat_hbm, flat),
                (wet_hbm, wet),
                (counts_hbm, counts),
                (settling_hbm, settling),
                (source_hbm, source),
                (tiles_hbm, tiles),
            )
        )
    ]
    for load in loads:
        load.start()

    crossed = v + 1 - 2 * core
    front = {"horiz": ahead, "vert": crossed}
    back = {"horiz": behind, "vert": crossed}

    barrier = pltpu.get_barrier_semaphore()
    for dy, dx, dc in ALL:
        pl.semaphore_signal(
            barrier, inc=1, device_id=target(dy, dx, dc), device_id_type=MESH
        )

    @pl.when(has_ahead)
    def _():
        pl.semaphore_signal(barrier, inc=1, device_id=front, device_id_type=MESH)

    @pl.when(has_behind)
    def _():
        pl.semaphore_signal(barrier, inc=1, device_id=back, device_id_type=MESH)

    near_at = jnp.where(even, 2 * blk, 0)
    far_at = jnp.where(even, 0, 2 * blk)

    def copy_to(src, dst, send, recv, where):
        return pltpu.make_async_remote_copy(
            src_ref=src,
            dst_ref=dst,
            send_sem=send,
            recv_sem=recv,
            device_id=where,
            device_id_type=MESH,
        )

    def remote(src, dst, p, q, kind, where):
        return copy_to(
            src, dst, send_sem.at[p, q, kind], recv_sem.at[p, q, kind], where
        )

    def first_copy(q, n):
        dy, dx, dc = ALL[n]
        mine = gath.at[0, q, 0, pl.ds(lev_dev * v, lev_dev)]
        return copy_to(
            other.at[q] if (dx + dc) % 2 else mine,
            gath.at[0, q, dy, pl.ds(lev_dev * v, lev_dev)],
            first_send.at[q, n],
            first_recv.at[q, n],
            target(dy, dx, dc),
        )

    def first_all(q, sending, act):
        for n, (dy, dx, dc) in enumerate(ALL):
            if not dx:
                act(first_copy(q, n))
                continue
            wanted = central if sending or dc else ~central

            @pl.when(wanted)
            def _():
                act(first_copy(q, n))

    def step_copy(p, q, n):
        dy, dx, dc = SAME[n]
        mine = gath.at[p % 2, q, 0, pl.ds(lev_chip * chip, lev_chip)]
        theirs = gath.at[p % 2, q, dy, pl.ds(lev_chip * chip, lev_chip)]
        return remote(mine, theirs, p, q, n, target(dy, dx, dc))

    def step_copies(p, q):
        kinds = (2,) if p == STEPS else (0, 1, 2)
        return [step_copy(p, q, n) for n in kinds]

    def block(p, q, at):
        return halos[p % 2 * Q + q].at[pl.ds(at, blk)]

    def front_copy(p, q):
        return remote(block(p, q, near_at), block(p, q, far_at), p, q, 3, front)

    def last_copies(q):
        theirs = lev_dev * (v + 1 - 2 * core) - base
        halo = halos[STEPS % 2 * Q + q]
        return [
            copy_to(
                halo.at[pl.ds(blk + t * window + theirs, lev_dev)],
                final.at[part * Q + q, t],
                last_send.at[q, t],
                last_recv.at[q, t],
                vert(1),
            )
            for t in range(tiles_dev)
        ]

    def pair_copies():
        mine = weights.at[pl.ds(lev_dev * core, lev_dev)]
        cols = cols_v.at[core]
        return [
            copy_to(cols, cols, pair_send.at[0], pair_recv.at[0], vert(1)),
            copy_to(mine, mine, pair_send.at[1], pair_recv.at[1], vert(1)),
        ]

    def load_first(q):
        for level in range(lev_dev):
            for t in range(tiles_dev):
                ours = pl.ds(pl.multiple_of(part * half + q * ch, ch), ch)
                theirs = pl.ds(pl.multiple_of((1 - part) * half + q * ch, ch), ch)
                gath[0, q, 0, lev_dev * v + level, t] = turned[level, t, ours, :]
                other[q, level, t] = turned[level, t, theirs, :]

    def explicit(p, q):
        for level in range(lev_chip):
            for t in range(tiles_dev):
                picked = jnp.concatenate(
                    [
                        halos[(p - 1) % 2 * Q + q][pos[level, t * slots + j]]
                        for j in range(slots)
                    ],
                    axis=1,
                )
                flow = jnp.dot(
                    picked, weights[level, t], preferred_element_type=F32
                )
                if level == 0:
                    ours = pl.ds(pl.multiple_of(part * half + q * ch, ch), ch)
                    flow = flow + src_t[t, ours, :]
                gath[p % 2, q, 0, lev_chip * chip + level, t] = flow.astype(BF16)

    def stage_a(p, q):
        if p == 0:
            first_all(q, True, lambda copy: copy.start())
            return
        if p == 1:
            first_all(q, True, lambda copy: copy.wait_send())
        else:
            for copy in step_copies(p - 1, q):
                copy.wait_send()

        @pl.when(has_behind)
        def _():
            front_copy(p - 1, q).wait_recv()

        explicit(p, q)
        for copy in step_copies(p, q):
            copy.start()

    def solve(p, q, which):
        par = p % 2
        halo = halos[par * Q + q]
        at0 = near_at if which else blk
        if p == 0:
            for t in range(tiles_dev):
                for k in range(window):
                    halo[at0 + t * window + k] = gath[par, q, which, base + k, t]
            return
        rows = 16

        for t in range(tiles_dev):
            for i in range(ch // rows):
                at = slice(i * rows, (i + 1) * rows)
                loaded = [
                    gath[par, q, which, m, t, at, :].astype(F32) for m in range(levels)
                ]
                start = part * half + q * ch + i * rows
                rate = fall[pl.ds(pl.multiple_of(start, rows), rows), :]
                stay = 1.0 - rate
                above = None
                for k in range(window + 1):
                    mixed = None
                    for m in range(levels):
                        r = k * levels + m
                        term = a_win[which, t, r : r + 1, :] * loaded[m]
                        mixed = term if m == 0 else mixed + term
                    if k:
                        settled = stay * mixed + rate * above
                        wet = w_win[which, t, k - 1 : k, :]
                        halo[at0 + t * window + k - 1, at, :] = (wet * settled).astype(
                            BF16
                        )
                    above = mixed

    def stage_b(p, q):
        if p == 0:
            first_all(q, False, lambda copy: copy.wait_recv())
        elif p < STEPS:
            step_copy(p, q, 0).wait_recv()
            step_copy(p, q, 1).wait_recv()
        if p:

            @pl.when(has_ahead)
            def _():
                front_copy(p - 1, q).wait_send()

        if p < STEPS:
            solve(p, q, 1)

            @pl.when(has_ahead)
            def _():
                front_copy(p, q).start()

        if p:
            step_copy(p, q, 2).wait_recv()
        solve(p, q, 0)
        if p == STEPS:
            for copy in last_copies(q):
                copy.start()

    def ops_copy(n):
        dy, dx, dc = SAME[n]
        return copy_to(
            extra, ops.at[dy, v], ops_send.at[n], ops_recv.at[n], target(dy, dx, dc)
        )

    def pass_copies():
        across = v_size - 1 - v
        return [
            copy_to(
                ops.at[dy, at],
                ops.at[dy, at],
                pass_send.at[dy, n],
                pass_recv.at[dy, n],
                vert(1),
            )
            for dy in range(2)
            for n, at in enumerate((v, across))
        ]

    def pack():
        rows = levels * levels // 2
        extra[:rows, :] = jnp.concatenate([flat[:rows, :], flat[rows:, :]], axis=1)
        extra[rows:, :] = jnp.zeros((8, size), F32)
        for level in range(lev_dev):
            for t in range(tiles_dev):
                at = rows + level * tiles_dev + t
                extra[at : at + 1, :] = wet[
                    level : level + 1, t * size : (t + 1) * size
                ].astype(F32)
        ops[0, v] = extra[...]

    def prepare():
        for level in range(lev_dev):
            for t in range(tiles_dev):
                for j in range(slots):
                    live = (j < counts[level, t]).astype(F32)
                    weights[lev_dev * core + level, t, j * size : (j + 1) * size, :] = (
                        tiles[level, t, j].astype(F32).T * live
                    ).astype(BF16)

    def prepare_more():
        on_top = (chip == 0).astype(F32)
        for t in range(tiles_dev):
            src_t[t] = source[t * size : (t + 1) * size, :].astype(F32).T * on_top
        fall[...] = jnp.broadcast_to(settling[...], (size, classes)).T

    def positions():
        local = pltpu.make_async_copy(cols_v, cols_s, local_sem)
        local.start()
        local.wait()
        last = 3 * blk - 1
        for level in range(lev_chip):
            for n in range(tiles_dev * slots):
                column = cols_s[
                    level // lev_dev, level % lev_dev, n // slots, n % slots
                ]
                row = lax.div(column, h_tiles) - base
                across = lax.rem(column, h_tiles) - tiles_dev * h + REACH
                pos[level, n] = jnp.clip(across * window + row, 0, last)

    def operators():
        rows = levels * levels // 2
        for which in range(2):
            for t in range(tiles_dev):
                a = ops[which, 2 * t, :rows, :]
                b = ops[which, 2 * t + 1, :rows, :]
                on_left = lax.broadcasted_iota(jnp.int32, a.shape, 1) < size // 2
                a_full[:levels, :] = jnp.zeros((levels, size), F32)
                a_full[levels : levels + rows, :] = jnp.where(
                    on_left, a, pltpu.roll(b, size // 2, 1)
                )
                a_full[levels + rows :, :] = jnp.where(
                    on_left, pltpu.roll(a, size // 2, 1), b
                )
                for k in range(window + 1):
                    level = base + k - 1
                    row = pl.ds(pl.multiple_of((level + 1) * levels, levels), levels)
                    a_win[which, t, k * levels : (k + 1) * levels, :] = a_full[row, :]
                    if k:
                        w_win[which, t, k - 1 : k, :] = ops[
                            which,
                            level // lev_dev,
                            pl.ds(rows + lax.rem(level, lev_dev) * tiles_dev + t, 1),
                            :,
                        ]

    for level in range(lev_dev):
        for t in range(tiles_dev):
            if level == t == 0:
                loads[0].wait()
            turned[level, t] = tracer[level, t * size : (t + 1) * size, :].T
    for q in range(Q):
        load_first(q)
    count = len(ALL) + has_ahead.astype(jnp.int32) + has_behind.astype(jnp.int32)
    pl.semaphore_wait(barrier, count)
    for q in range(Q):
        stage_a(0, q)
    for load in loads[1:-1]:
        load.wait()
    pair = pair_copies()
    pair[0].start()
    pack()
    for n in range(len(SAME)):
        ops_copy(n).start()
    loads[-1].wait()
    prepare()
    pair[1].start()
    for q in range(Q):
        stage_b(0, q)
    for n in range(len(SAME)):
        ops_copy(n).wait()
    for copy in pass_copies():
        copy.start()
    prepare_more()
    pair[0].wait()
    positions()
    pair[1].wait()
    for q in range(Q):
        stage_a(1, q)
    for copy in pass_copies():
        copy.wait()
    operators()
    for late, p, q in ORDER:
        if late:
            stage_a(p + 1, q)
        else:
            stage_b(p, q)
    mine = lev_dev * v - base
    for q in range(Q):
        for t in range(tiles_dev):
            for level in range(lev_dev):
                final[part * Q + q, t, level] = halos[STEPS % 2 * Q + q][
                    blk + t * window + mine + level
                ]
    for q in range(Q):
        for copy in last_copies(q):
            copy.wait_recv()
    for level in range(lev_dev):
        for t in range(tiles_dev):
            whole = jnp.concatenate(
                [final[i, t, level] for i in range(2 * Q)], axis=0
            )
            out[level, t * size : (t + 1) * size, :] = whole.T
    for q in range(Q):
        for copy in step_copies(STEPS, q) + last_copies(q):
            copy.wait_send()


def on_device(h_size, v_size, tracer, tiles, columns, counts, source, implicit, settling, wet):
    lev_dev, cells_dev, classes = tracer.shape
    slots, size = tiles.shape[2], tiles.shape[3]
    tiles_dev = cells_dev // size
    levels = implicit.shape[1]
    share = implicit.shape[0]
    window = lev_dev + 2 * REACH
    assert lev_dev == 2 and tiles_dev == 2 and v_size == 4 and h_size % 2 == 0
    ch = classes // 2 // Q
    flat = implicit.reshape(share, levels * levels).T
    settling = settling.reshape(1, classes)
    extra = (levels * levels // 2 + 8, size)
    hbm = pl.BlockSpec(memory_space=pl.ANY)
    vm = pl.BlockSpec(memory_space=pltpu.VMEM)
    phases = STEPS + 1
    dma = pltpu.SemaphoreType.DMA
    return pl.pallas_call(
        functools.partial(kernel, h_size, v_size),
        out_shape=jax.ShapeDtypeStruct(tracer.shape, tracer.dtype),
        in_specs=[hbm] * 8,
        out_specs=vm,
        scratch_shapes=[
            pltpu.VMEM(tracer.shape, BF16),
            pltpu.VMEM(tiles.shape, BF16),
            pltpu.SMEM(counts.shape, jnp.int32),
            pltpu.VMEM(source.shape, BF16),
            pltpu.VMEM(flat.shape, F32),
            pltpu.VMEM(settling.shape, F32),
            pltpu.VMEM(wet.shape, jnp.int32),
            pltpu.VMEM(extra, F32),
            pltpu.VMEM((2 * lev_dev, tiles_dev, slots * size, size), BF16),
            pltpu.VMEM((lev_dev, tiles_dev, classes, size), BF16),
            pltpu.VMEM((2, Q, 2, levels, tiles_dev, ch, size), BF16),
            pltpu.VMEM((Q, lev_dev, tiles_dev, ch, size), BF16),
            pltpu.VMEM((2 * Q, tiles_dev, lev_dev, ch, size), BF16),
            pltpu.VMEM((tiles_dev, classes, size), F32),
            pltpu.VMEM((classes, size), F32),
            pltpu.VMEM((2, v_size) + extra, F32),
            pltpu.VMEM(((levels + 1) * levels, size), F32),
            pltpu.VMEM((2, tiles_dev, (window + 1) * levels, size), F32),
            pltpu.VMEM((2, tiles_dev, 8, size), F32),
            pltpu.VMEM((2,) + columns.shape, jnp.int32),
            pltpu.SMEM((2,) + columns.shape, jnp.int32),
            pltpu.SMEM((2 * lev_dev, tiles_dev * slots), jnp.int32),
            dma((phases, Q, 4)),
            dma((phases, Q, 4)),
            dma((Q, len(ALL))),
            dma((Q, len(ALL))),
            dma((Q, tiles_dev)),
            dma((Q, tiles_dev)),
            dma((len(SAME),)),
            dma((len(SAME),)),
            dma((2, 2)),
            dma((2, 2)),
            dma((2,)),
            dma((2,)),
            dma(()),
            dma((8,)),
        ]
        + [pltpu.VMEM((3 * tiles_dev * window, ch, size), BF16)] * (2 * Q),
        compiler_params=pltpu.CompilerParams(
            collective_id=0, has_side_effects=True, vmem_limit_bytes=32 * 2**20
        ),
    )(
        *(
            pltpu.with_memory_space_constraint(operand, pltpu.HBM)
            for operand in (
                tracer, tiles, columns, counts, source, flat, settling, wet
            )
        )
    )


def solution(mesh):
    placed = (
        P("vert", "horiz", None),
        P("vert", "horiz", None, None, None),
        P("vert", "horiz", None),
        P("vert", "horiz"),
        P("horiz", None),
        P(("horiz", "vert"), None, None),
        P(),
        P("vert", "horiz"),
    )
    body = functools.partial(on_device, mesh.shape["horiz"], mesh.shape["vert"])
    return jax.shard_map(
        body, mesh=mesh, in_specs=placed, out_specs=P("vert", "horiz", None), check_vma=False
    )
```

```python
import functools

import jax
import jax.numpy as jnp
from jax import lax
from jax.experimental import pallas as pl
from jax.experimental.pallas import tpu as pltpu
from jax.sharding import PartitionSpec as P

REACH = 2
STEPS = 4
Q = 4
ORDER = [
    (late, p, q)
    for when, late, p, q in sorted(
        (6.8 * p + 3.0 * late + 1.4 * q, late, p, q)
        for p in range(1, STEPS + 1)
        for late in range(2)
        for q in range(Q)
        if p + late <= STEPS
    )
]
MESH = pl.DeviceIdType.MESH
ALL = ((1, 1, 1), (1, 1, 0), (1, 0, 0), (1, 0, 1), (0, 1, 1), (0, 1, 0), (0, 0, 1))
SAME = ((1, 1, 1), (1, 0, 0), (0, 1, 1))
F32 = jnp.float32
BF16 = jnp.bfloat16


def kernel(
    h_size,
    v_size,
    tracer_hbm,
    tiles_hbm,
    columns_hbm,
    counts_hbm,
    source_hbm,
    flat_hbm,
    settling_hbm,
    wet_hbm,
    out,
    tracer,
    tiles,
    counts,
    source,
    flat,
    settling,
    wet,
    extra,
    weights,
    turned,
    gath,
    other,
    final,
    src_t,
    fall,
    ops,
    a_full,
    a_win,
    w_win,
    cols_v,
    cols_s,
    pos,
    send_sem,
    recv_sem,
    first_send,
    first_recv,
    last_send,
    last_recv,
    ops_send,
    ops_recv,
    pass_send,
    pass_recv,
    pair_send,
    pair_recv,
    local_sem,
    load_sem,
    *halos,
):
    lev_dev, cells_dev, classes = tracer.shape
    slots, size = tiles.shape[2], tiles.shape[3]
    tiles_dev = cells_dev // size
    window = lev_dev + 2 * REACH
    levels = lev_dev * v_size
    lev_chip = 2 * lev_dev
    h_tiles = h_size * tiles_dev
    half = classes // 2
    ch = half // Q
    blk = tiles_dev * window
    h = lax.axis_index("horiz")
    v = lax.axis_index("vert")
    even = lax.rem(h, 2) == 0
    core = lax.rem(v, 2)
    chip = v // 2
    base = 2 * chip
    partner = jnp.where(even, h + 1, h - 1)
    ahead = jnp.where(even, h + 2, h - 2)
    behind = jnp.where(even, h - 2, h + 2)
    has_ahead = (ahead >= 0) & (ahead < h_size)
    has_behind = (behind >= 0) & (behind < h_size)
    part = lax.rem(core + chip + h // 2, 2)
    central = lax.rem(core + chip, 2) == 1

    def target(dy, dx, dc):
        flipped = v
        if dc:
            flipped = flipped + 1 - 2 * core
        if dx:
            flipped = lax.rem(flipped + 2, 4)
        return {"horiz": partner if dy else h, "vert": flipped}

    def vert(d):
        return target(0, d // 2, d % 2)

    crossed = v + 1 - 2 * core
    front = {"horiz": ahead, "vert": crossed}
    back = {"horiz": behind, "vert": crossed}

    barrier = pltpu.get_barrier_semaphore()
    for dy, dx, dc in ALL:
        pl.semaphore_signal(
            barrier, inc=1, device_id=target(dy, dx, dc), device_id_type=MESH
        )

    @pl.when(has_ahead)
    def _():
        pl.semaphore_signal(barrier, inc=1, device_id=front, device_id_type=MESH)

    @pl.when(has_behind)
    def _():
        pl.semaphore_signal(barrier, inc=1, device_id=back, device_id_type=MESH)

    loads = [
        pltpu.make_async_copy(src, dst, load_sem.at[n])
        for n, (src, dst) in enumerate(
            (
                (tracer_hbm, tracer),
                (columns_hbm, cols_v.at[core]),
                (flat_hbm, flat),
                (wet_hbm, wet),
                (counts_hbm, counts),
                (settling_hbm, settling),
                (source_hbm, source),
                (tiles_hbm, tiles),
            )
        )
    ]
    for load in loads:
        load.start()

    near_at = jnp.where(even, 2 * blk, 0)
    far_at = jnp.where(even, 0, 2 * blk)

    def copy_to(src, dst, send, recv, where):
        return pltpu.make_async_remote_copy(
            src_ref=src,
            dst_ref=dst,
            send_sem=send,
            recv_sem=recv,
            device_id=where,
            device_id_type=MESH,
        )

    def remote(src, dst, p, q, kind, where):
        return copy_to(
            src, dst, send_sem.at[p, q, kind], recv_sem.at[p, q, kind], where
        )

    def first_copy(q, n):
        dy, dx, dc = ALL[n]
        mine = gath.at[0, q, 0, pl.ds(lev_dev * v, lev_dev)]
        return copy_to(
            other.at[q] if (dx + dc) % 2 else mine,
            gath.at[0, q, dy, pl.ds(lev_dev * v, lev_dev)],
            first_send.at[q, n],
            first_recv.at[q, n],
            target(dy, dx, dc),
        )

    def first_all(q, sending, act):
        for n, (dy, dx, dc) in enumerate(ALL):
            if not dx:
                act(first_copy(q, n))
                continue
            wanted = central if sending or dc else ~central

            @pl.when(wanted)
            def _():
                act(first_copy(q, n))

    def step_copy(p, q, n):
        dy, dx, dc = SAME[n]
        mine = gath.at[p % 2, q, 0, pl.ds(lev_chip * chip, lev_chip)]
        theirs = gath.at[p % 2, q, dy, pl.ds(lev_chip * chip, lev_chip)]
        return remote(mine, theirs, p, q, n, target(dy, dx, dc))

    def step_copies(p, q):
        kinds = (2,) if p == STEPS else (0, 1, 2)
        return [step_copy(p, q, n) for n in kinds]

    def block(p, q, at):
        return halos[p % 2 * Q + q].at[pl.ds(at, blk)]

    def front_copy(p, q):
        return remote(block(p, q, near_at), block(p, q, far_at), p, q, 3, front)

    def last_copies(q):
        theirs = lev_dev * (v + 1 - 2 * core) - base
        halo = halos[STEPS % 2 * Q + q]
        return [
            copy_to(
                halo.at[pl.ds(blk + t * window + theirs, lev_dev)],
                final.at[part * Q + q, t],
                last_send.at[q, t],
                last_recv.at[q, t],
                vert(1),
            )
            for t in range(tiles_dev)
        ]

    def pair_copies():
        mine = weights.at[pl.ds(lev_dev * core, lev_dev)]
        cols = cols_v.at[core]
        return [
            copy_to(cols, cols, pair_send.at[0], pair_recv.at[0], vert(1)),
            copy_to(mine, mine, pair_send.at[1], pair_recv.at[1], vert(1)),
        ]

    def load_first(q):
        for level in range(lev_dev):
            for t in range(tiles_dev):
                ours = pl.ds(pl.multiple_of(part * half + q * ch, ch), ch)
                theirs = pl.ds(pl.multiple_of((1 - part) * half + q * ch, ch), ch)
                gath[0, q, 0, lev_dev * v + level, t] = turned[level, t, ours, :]
                other[q, level, t] = turned[level, t, theirs, :]

    def explicit(p, q):
        for level in range(lev_chip):
            for t in range(tiles_dev):
                picked = jnp.concatenate(
                    [
                        halos[(p - 1) % 2 * Q + q][pos[level, t * slots + j]]
                        for j in range(slots)
                    ],
                    axis=1,
                )
                flow = jnp.dot(
                    picked, weights[level, t], preferred_element_type=F32
                )
                if level == 0:
                    ours = pl.ds(pl.multiple_of(part * half + q * ch, ch), ch)
                    flow = flow + src_t[t, ours, :]
                gath[p % 2, q, 0, lev_chip * chip + level, t] = flow.astype(BF16)

    def stage_a(p, q):
        if p == 0:
            first_all(q, True, lambda copy: copy.start())
            return
        if p == 1:
            first_all(q, True, lambda copy: copy.wait_send())
        else:
            for copy in step_copies(p - 1, q):
                copy.wait_send()

        @pl.when(has_behind)
        def _():
            front_copy(p - 1, q).wait_recv()

        explicit(p, q)
        for copy in step_copies(p, q):
            copy.start()

    def solve(p, q, which):
        par = p % 2
        halo = halos[par * Q + q]
        at0 = near_at if which else blk
        if p == 0:
            for t in range(tiles_dev):
                for k in range(window):
                    halo[at0 + t * window + k] = gath[par, q, which, base + k, t]
            return
        rows = 16

        for t in range(tiles_dev):
            for i in range(ch // rows):
                at = slice(i * rows, (i + 1) * rows)
                loaded = [
                    gath[par, q, which, m, t, at, :].astype(F32) for m in range(levels)
                ]
                start = part * half + q * ch + i * rows
                rate = fall[pl.ds(pl.multiple_of(start, rows), rows), :]
                stay = 1.0 - rate
                above = None
                for k in range(window + 1):
                    mixed = None
                    for m in range(levels):
                        r = k * levels + m
                        term = a_win[which, t, r : r + 1, :] * loaded[m]
                        mixed = term if m == 0 else mixed + term
                    if k:
                        settled = stay * mixed + rate * above
                        wet = w_win[which, t, k - 1 : k, :]
                        halo[at0 + t * window + k - 1, at, :] = (wet * settled).astype(
                            BF16
                        )
                    above = mixed

    def stage_b(p, q):
        if p == 0:
            first_all(q, False, lambda copy: copy.wait_recv())
        elif p < STEPS:
            step_copy(p, q, 0).wait_recv()
            step_copy(p, q, 1).wait_recv()
        if p:

            @pl.when(has_ahead)
            def _():
                front_copy(p - 1, q).wait_send()

        if p < STEPS:
            solve(p, q, 1)

            @pl.when(has_ahead)
            def _():
                front_copy(p, q).start()

        if p:
            step_copy(p, q, 2).wait_recv()
        solve(p, q, 0)
        if p == STEPS:
            for copy in last_copies(q):
                copy.start()

    def ops_copy(n):
        dy, dx, dc = SAME[n]
        return copy_to(
            extra, ops.at[dy, v], ops_send.at[n], ops_recv.at[n], target(dy, dx, dc)
        )

    def pass_copies():
        across = v_size - 1 - v
        return [
            copy_to(
                ops.at[dy, at],
                ops.at[dy, at],
                pass_send.at[dy, n],
                pass_recv.at[dy, n],
                vert(1),
            )
            for dy in range(2)
            for n, at in enumerate((v, across))
        ]

    def pack():
        rows = levels * levels // 2
        extra[:rows, :] = jnp.concatenate([flat[:rows, :], flat[rows:, :]], axis=1)
        extra[rows:, :] = jnp.zeros((8, size), F32)
        for level in range(lev_dev):
            for t in range(tiles_dev):
                at = rows + level * tiles_dev + t
                extra[at : at + 1, :] = wet[
                    level : level + 1, t * size : (t + 1) * size
                ].astype(F32)
        ops[0, v] = extra[...]

    def prepare():
        for level in range(lev_dev):
            for t in range(tiles_dev):
                for j in range(slots):
                    live = (j < counts[level, t]).astype(F32)
                    weights[lev_dev * core + level, t, j * size : (j + 1) * size, :] = (
                        tiles[level, t, j].astype(F32).T * live
                    ).astype(BF16)

    def prepare_more():
        on_top = (chip == 0).astype(F32)
        for t in range(tiles_dev):
            src_t[t] = source[t * size : (t + 1) * size, :].astype(F32).T * on_top
        fall[...] = jnp.broadcast_to(settling[...], (size, classes)).T

    def positions():
        local = pltpu.make_async_copy(cols_v, cols_s, local_sem)
        local.start()
        local.wait()
        last = 3 * blk - 1
        for level in range(lev_chip):
            for n in range(tiles_dev * slots):
                column = cols_s[
                    level // lev_dev, level % lev_dev, n // slots, n % slots
                ]
                row = lax.div(column, h_tiles) - base
                across = lax.rem(column, h_tiles) - tiles_dev * h + REACH
                pos[level, n] = jnp.clip(across * window + row, 0, last)

    def operators():
        rows = levels * levels // 2
        for which in range(2):
            for t in range(tiles_dev):
                a = ops[which, 2 * t, :rows, :]
                b = ops[which, 2 * t + 1, :rows, :]
                on_left = lax.broadcasted_iota(jnp.int32, a.shape, 1) < size // 2
                a_full[:levels, :] = jnp.zeros((levels, size), F32)
                a_full[levels : levels + rows, :] = jnp.where(
                    on_left, a, pltpu.roll(b, size // 2, 1)
                )
                a_full[levels + rows :, :] = jnp.where(
                    on_left, pltpu.roll(a, size // 2, 1), b
                )
                for k in range(window + 1):
                    level = base + k - 1
                    row = pl.ds(pl.multiple_of((level + 1) * levels, levels), levels)
                    a_win[which, t, k * levels : (k + 1) * levels, :] = a_full[row, :]
                    if k:
                        w_win[which, t, k - 1 : k, :] = ops[
                            which,
                            level // lev_dev,
                            pl.ds(rows + lax.rem(level, lev_dev) * tiles_dev + t, 1),
                            :,
                        ]

    for level in range(lev_dev):
        for t in range(tiles_dev):
            if level == t == 0:
                loads[0].wait()
            turned[level, t] = tracer[level, t * size : (t + 1) * size, :].T
    for q in range(Q):
        load_first(q)
    count = len(ALL) + has_ahead.astype(jnp.int32) + has_behind.astype(jnp.int32)
    pl.semaphore_wait(barrier, count)
    for q in range(Q):
        stage_a(0, q)
    for load in loads[1:-1]:
        load.wait()
    pair = pair_copies()
    pair[0].start()
    pack()
    for n in range(len(SAME)):
        ops_copy(n).start()
    loads[-1].wait()
    prepare()
    pair[1].start()
    stage_b(0, 0)
    prepare_more()
    pair[0].wait()
    positions()
    for q in range(1, Q):
        stage_b(0, q)
    pair[1].wait()
    stage_a(1, 0)
    for n in range(len(SAME)):
        ops_copy(n).wait()
    for copy in pass_copies():
        copy.start()
    for q in range(1, Q):
        stage_a(1, q)
    for copy in pass_copies():
        copy.wait()
    operators()
    for late, p, q in ORDER:
        if late:
            stage_a(p + 1, q)
        else:
            stage_b(p, q)
    mine = lev_dev * v - base
    for q in range(Q):
        for t in range(tiles_dev):
            for level in range(lev_dev):
                final[part * Q + q, t, level] = halos[STEPS % 2 * Q + q][
                    blk + t * window + mine + level
                ]
    for q in range(Q):
        for copy in last_copies(q):
            copy.wait_recv()
    for level in range(lev_dev):
        for t in range(tiles_dev):
            whole = jnp.concatenate(
                [final[i, t, level] for i in range(2 * Q)], axis=0
            )
            out[level, t * size : (t + 1) * size, :] = whole.T
    for q in range(Q):
        for copy in step_copies(STEPS, q) + last_copies(q):
            copy.wait_send()


def on_device(h_size, v_size, tracer, tiles, columns, counts, source, implicit, settling, wet):
    lev_dev, cells_dev, classes = tracer.shape
    slots, size = tiles.shape[2], tiles.shape[3]
    tiles_dev = cells_dev // size
    levels = implicit.shape[1]
    share = implicit.shape[0]
    window = lev_dev + 2 * REACH
    assert lev_dev == 2 and tiles_dev == 2 and v_size == 4 and h_size % 2 == 0
    ch = classes // 2 // Q
    flat = implicit.reshape(share, levels * levels).T
    settling = settling.reshape(1, classes)
    extra = (levels * levels // 2 + 8, size)
    hbm = pl.BlockSpec(memory_space=pl.ANY)
    vm = pl.BlockSpec(memory_space=pltpu.VMEM)
    phases = STEPS + 1
    dma = pltpu.SemaphoreType.DMA
    return pl.pallas_call(
        functools.partial(kernel, h_size, v_size),
        out_shape=jax.ShapeDtypeStruct(tracer.shape, tracer.dtype),
        in_specs=[hbm] * 8,
        out_specs=vm,
        scratch_shapes=[
            pltpu.VMEM(tracer.shape, BF16),
            pltpu.VMEM(tiles.shape, BF16),
            pltpu.SMEM(counts.shape, jnp.int32),
            pltpu.VMEM(source.shape, BF16),
            pltpu.VMEM(flat.shape, F32),
            pltpu.VMEM(settling.shape, F32),
            pltpu.VMEM(wet.shape, jnp.int32),
            pltpu.VMEM(extra, F32),
            pltpu.VMEM((2 * lev_dev, tiles_dev, slots * size, size), BF16),
            pltpu.VMEM((lev_dev, tiles_dev, classes, size), BF16),
            pltpu.VMEM((2, Q, 2, levels, tiles_dev, ch, size), BF16),
            pltpu.VMEM((Q, lev_dev, tiles_dev, ch, size), BF16),
            pltpu.VMEM((2 * Q, tiles_dev, lev_dev, ch, size), BF16),
            pltpu.VMEM((tiles_dev, classes, size), F32),
            pltpu.VMEM((classes, size), F32),
            pltpu.VMEM((2, v_size) + extra, F32),
            pltpu.VMEM(((levels + 1) * levels, size), F32),
            pltpu.VMEM((2, tiles_dev, (window + 1) * levels, size), F32),
            pltpu.VMEM((2, tiles_dev, 8, size), F32),
            pltpu.VMEM((2,) + columns.shape, jnp.int32),
            pltpu.SMEM((2,) + columns.shape, jnp.int32),
            pltpu.SMEM((2 * lev_dev, tiles_dev * slots), jnp.int32),
            dma((phases, Q, 4)),
            dma((phases, Q, 4)),
            dma((Q, len(ALL))),
            dma((Q, len(ALL))),
            dma((Q, tiles_dev)),
            dma((Q, tiles_dev)),
            dma((len(SAME),)),
            dma((len(SAME),)),
            dma((2, 2)),
            dma((2, 2)),
            dma((2,)),
            dma((2,)),
            dma(()),
            dma((8,)),
        ]
        + [pltpu.VMEM((3 * tiles_dev * window, ch, size), BF16)] * (2 * Q),
        compiler_params=pltpu.CompilerParams(
            collective_id=0, has_side_effects=True, vmem_limit_bytes=32 * 2**20
        ),
    )(
        *(
            pltpu.with_memory_space_constraint(operand, pltpu.HBM)
            for operand in (
                tracer, tiles, columns, counts, source, flat, settling, wet
            )
        )
    )


def solution(mesh):
    placed = (
        P("vert", "horiz", None),
        P("vert", "horiz", None, None, None),
        P("vert", "horiz", None),
        P("vert", "horiz"),
        P("horiz", None),
        P(("horiz", "vert"), None, None),
        P(),
        P("vert", "horiz"),
    )
    body = functools.partial(on_device, mesh.shape["horiz"], mesh.shape["vert"])
    return jax.shard_map(
        body, mesh=mesh, in_specs=placed, out_specs=P("vert", "horiz", None), check_vma=False
    )
```

```python
import functools

import jax
import jax.numpy as jnp
from jax import lax
from jax.experimental import pallas as pl
from jax.experimental.pallas import tpu as pltpu
from jax.sharding import PartitionSpec as P

REACH = 2
STEPS = 4
Q = 4
ORDER = [
    (late, p, q)
    for when, late, p, q in sorted(
        (6.8 * p + 3.0 * late + 1.4 * q, late, p, q)
        for p in range(1, STEPS + 1)
        for late in range(2)
        for q in range(Q)
        if p + late <= STEPS
    )
]
MESH = pl.DeviceIdType.MESH
ALL = ((1, 1, 1), (1, 1, 0), (1, 0, 0), (1, 0, 1), (0, 1, 1), (0, 1, 0), (0, 0, 1))
SAME = ((1, 1, 1), (1, 0, 0), (0, 1, 1))
F32 = jnp.float32
BF16 = jnp.bfloat16


def kernel(
    h_size,
    v_size,
    tracer_hbm,
    tiles_hbm,
    columns_hbm,
    counts_hbm,
    source_hbm,
    flat_hbm,
    settling_hbm,
    wet_hbm,
    out,
    tracer,
    tiles,
    counts,
    source,
    flat,
    settling,
    wet,
    extra,
    weights,
    turned,
    gath,
    other,
    final,
    src_t,
    fall,
    ops,
    a_full,
    a_win,
    w_win,
    cols_v,
    cols_s,
    pos,
    send_sem,
    recv_sem,
    first_send,
    first_recv,
    last_send,
    last_recv,
    ops_send,
    ops_recv,
    pass_send,
    pass_recv,
    pair_send,
    pair_recv,
    local_sem,
    load_sem,
    *halos,
):
    lev_dev, cells_dev, classes = tracer.shape
    slots, size = tiles.shape[2], tiles.shape[3]
    tiles_dev = cells_dev // size
    window = lev_dev + 2 * REACH
    levels = lev_dev * v_size
    lev_chip = 2 * lev_dev
    h_tiles = h_size * tiles_dev
    half = classes // 2
    ch = half // Q
    blk = tiles_dev * window
    h = lax.axis_index("horiz")
    v = lax.axis_index("vert")
    even = lax.rem(h, 2) == 0
    core = lax.rem(v, 2)
    chip = v // 2
    base = 2 * chip
    partner = jnp.where(even, h + 1, h - 1)
    ahead = jnp.where(even, h + 2, h - 2)
    behind = jnp.where(even, h - 2, h + 2)
    has_ahead = (ahead >= 0) & (ahead < h_size)
    has_behind = (behind >= 0) & (behind < h_size)
    part = lax.rem(core + chip + h // 2, 2)
    central = lax.rem(core + chip, 2) == 1

    def target(dy, dx, dc):
        flipped = v
        if dc:
            flipped = flipped + 1 - 2 * core
        if dx:
            flipped = lax.rem(flipped + 2, 4)
        return {"horiz": partner if dy else h, "vert": flipped}

    def vert(d):
        return target(0, d // 2, d % 2)

    crossed = v + 1 - 2 * core
    front = {"horiz": ahead, "vert": crossed}
    back = {"horiz": behind, "vert": crossed}

    barrier = pltpu.get_barrier_semaphore()
    for dy, dx, dc in ALL:
        pl.semaphore_signal(
            barrier, inc=1, device_id=target(dy, dx, dc), device_id_type=MESH
        )

    @pl.when(has_ahead)
    def _():
        pl.semaphore_signal(barrier, inc=1, device_id=front, device_id_type=MESH)

    @pl.when(has_behind)
    def _():
        pl.semaphore_signal(barrier, inc=1, device_id=back, device_id_type=MESH)

    loads = [
        pltpu.make_async_copy(src, dst, load_sem.at[n])
        for n, (src, dst) in enumerate(
            (
                (tracer_hbm, tracer),
                (columns_hbm, cols_v.at[core]),
                (flat_hbm, flat),
                (wet_hbm, wet),
                (counts_hbm, counts),
                (settling_hbm, settling),
                (source_hbm, source),
                (tiles_hbm, tiles),
            )
        )
    ]
    for load in loads:
        load.start()

    near_at = jnp.where(even, 2 * blk, 0)
    far_at = jnp.where(even, 0, 2 * blk)

    def copy_to(src, dst, send, recv, where):
        return pltpu.make_async_remote_copy(
            src_ref=src,
            dst_ref=dst,
            send_sem=send,
            recv_sem=recv,
            device_id=where,
            device_id_type=MESH,
        )

    def remote(src, dst, p, q, kind, where):
        return copy_to(
            src, dst, send_sem.at[p, q, kind], recv_sem.at[p, q, kind], where
        )

    def first_copy(q, n):
        dy, dx, dc = ALL[n]
        mine = gath.at[0, q, 0, pl.ds(lev_dev * v, lev_dev)]
        return copy_to(
            other.at[q] if (dx + dc) % 2 else mine,
            gath.at[0, q, dy, pl.ds(lev_dev * v, lev_dev)],
            first_send.at[q, n],
            first_recv.at[q, n],
            target(dy, dx, dc),
        )

    def first_all(q, sending, act):
        for n, (dy, dx, dc) in enumerate(ALL):
            if not dx:
                act(first_copy(q, n))
                continue
            wanted = central if sending or dc else ~central

            @pl.when(wanted)
            def _():
                act(first_copy(q, n))

    def step_copy(p, q, n):
        dy, dx, dc = SAME[n]
        mine = gath.at[p % 2, q, 0, pl.ds(lev_chip * chip, lev_chip)]
        theirs = gath.at[p % 2, q, dy, pl.ds(lev_chip * chip, lev_chip)]
        return remote(mine, theirs, p, q, n, target(dy, dx, dc))

    def step_copies(p, q):
        kinds = (2,) if p == STEPS else (0, 1, 2)
        return [step_copy(p, q, n) for n in kinds]

    def block(p, q, at):
        return halos[p % 2 * Q + q].at[pl.ds(at, blk)]

    def front_copy(p, q):
        return remote(block(p, q, near_at), block(p, q, far_at), p, q, 3, front)

    def last_copies(q):
        theirs = lev_dev * (v + 1 - 2 * core) - base
        halo = halos[STEPS % 2 * Q + q]
        return [
            copy_to(
                halo.at[pl.ds(blk + t * window + theirs, lev_dev)],
                final.at[part * Q + q, t],
                last_send.at[q, t],
                last_recv.at[q, t],
                vert(1),
            )
            for t in range(tiles_dev)
        ]

    def pair_copies():
        mine = weights.at[pl.ds(lev_dev * core, lev_dev)]
        cols = cols_v.at[core]
        return [
            copy_to(cols, cols, pair_send.at[0], pair_recv.at[0], vert(1)),
            copy_to(mine, mine, pair_send.at[1], pair_recv.at[1], vert(1)),
        ]

    def load_first(q):
        for level in range(lev_dev):
            for t in range(tiles_dev):
                ours = pl.ds(pl.multiple_of(part * half + q * ch, ch), ch)
                theirs = pl.ds(pl.multiple_of((1 - part) * half + q * ch, ch), ch)
                gath[0, q, 0, lev_dev * v + level, t] = turned[level, t, ours, :]
                other[q, level, t] = turned[level, t, theirs, :]

    def explicit(p, q):
        for level in range(lev_chip):
            for t in range(tiles_dev):
                picked = jnp.concatenate(
                    [
                        halos[(p - 1) % 2 * Q + q][pos[level, t * slots + j]]
                        for j in range(slots)
                    ],
                    axis=1,
                )
                flow = jnp.dot(
                    picked, weights[level, t], preferred_element_type=F32
                )
                if level == 0:
                    ours = pl.ds(pl.multiple_of(part * half + q * ch, ch), ch)
                    flow = flow + src_t[t, ours, :]
                gath[p % 2, q, 0, lev_chip * chip + level, t] = flow.astype(BF16)

    def stage_a(p, q):
        if p == 0:
            first_all(q, True, lambda copy: copy.start())
            return
        if p > 1:
            solve_own(p - 1, q)
        if p == 1:
            first_all(q, True, lambda copy: copy.wait_send())
        else:
            for copy in step_copies(p - 1, q):
                copy.wait_send()

        @pl.when(has_behind)
        def _():
            front_copy(p - 1, q).wait_recv()

        explicit(p, q)
        for copy in step_copies(p, q):
            copy.start()

    def solve(p, q, which):
        par = p % 2
        halo = halos[par * Q + q]
        at0 = near_at if which else blk
        if p == 0:
            for t in range(tiles_dev):
                for k in range(window):
                    halo[at0 + t * window + k] = gath[par, q, which, base + k, t]
            return
        rows = 16

        for t in range(tiles_dev):
            for i in range(ch // rows):
                at = slice(i * rows, (i + 1) * rows)
                loaded = [
                    gath[par, q, which, m, t, at, :].astype(F32) for m in range(levels)
                ]
                start = part * half + q * ch + i * rows
                rate = fall[pl.ds(pl.multiple_of(start, rows), rows), :]
                stay = 1.0 - rate
                above = None
                for k in range(window + 1):
                    mixed = None
                    for m in range(levels):
                        r = k * levels + m
                        term = a_win[which, t, r : r + 1, :] * loaded[m]
                        mixed = term if m == 0 else mixed + term
                    if k:
                        settled = stay * mixed + rate * above
                        wet = w_win[which, t, k - 1 : k, :]
                        halo[at0 + t * window + k - 1, at, :] = (wet * settled).astype(
                            BF16
                        )
                    above = mixed

    def solve_own(p, q):
        if p:
            step_copy(p, q, 2).wait_recv()
        solve(p, q, 0)

    def stage_b(p, q):
        if p == 0:
            first_all(q, False, lambda copy: copy.wait_recv())
        elif p < STEPS:
            step_copy(p, q, 0).wait_recv()
            step_copy(p, q, 1).wait_recv()
        if p:

            @pl.when(has_ahead)
            def _():
                front_copy(p - 1, q).wait_send()

        if p < STEPS:
            solve(p, q, 1)

            @pl.when(has_ahead)
            def _():
                front_copy(p, q).start()

        if p == 0 or p == STEPS:
            solve_own(p, q)
        if p == STEPS:
            for copy in last_copies(q):
                copy.start()

    def ops_copy(n):
        dy, dx, dc = SAME[n]
        return copy_to(
            extra, ops.at[dy, v], ops_send.at[n], ops_recv.at[n], target(dy, dx, dc)
        )

    def pass_copies():
        across = v_size - 1 - v
        return [
            copy_to(
                ops.at[dy, at],
                ops.at[dy, at],
                pass_send.at[dy, n],
                pass_recv.at[dy, n],
                vert(1),
            )
            for dy in range(2)
            for n, at in enumerate((v, across))
        ]

    def pack():
        rows = levels * levels // 2
        extra[:rows, :] = jnp.concatenate([flat[:rows, :], flat[rows:, :]], axis=1)
        extra[rows:, :] = jnp.zeros((8, size), F32)
        for level in range(lev_dev):
            for t in range(tiles_dev):
                at = rows + level * tiles_dev + t
                extra[at : at + 1, :] = wet[
                    level : level + 1, t * size : (t + 1) * size
                ].astype(F32)
        ops[0, v] = extra[...]

    def prepare():
        for level in range(lev_dev):
            for t in range(tiles_dev):
                for j in range(slots):
                    live = (j < counts[level, t]).astype(F32)
                    weights[lev_dev * core + level, t, j * size : (j + 1) * size, :] = (
                        tiles[level, t, j].astype(F32).T * live
                    ).astype(BF16)

    def prepare_more():
        on_top = (chip == 0).astype(F32)
        for t in range(tiles_dev):
            src_t[t] = source[t * size : (t + 1) * size, :].astype(F32).T * on_top
        fall[...] = jnp.broadcast_to(settling[...], (size, classes)).T

    def positions():
        local = pltpu.make_async_copy(cols_v, cols_s, local_sem)
        local.start()
        local.wait()
        last = 3 * blk - 1
        for level in range(lev_chip):
            for n in range(tiles_dev * slots):
                column = cols_s[
                    level // lev_dev, level % lev_dev, n // slots, n % slots
                ]
                row = lax.div(column, h_tiles) - base
                across = lax.rem(column, h_tiles) - tiles_dev * h + REACH
                pos[level, n] = jnp.clip(across * window + row, 0, last)

    def operators():
        rows = levels * levels // 2
        for which in range(2):
            for t in range(tiles_dev):
                a = ops[which, 2 * t, :rows, :]
                b = ops[which, 2 * t + 1, :rows, :]
                on_left = lax.broadcasted_iota(jnp.int32, a.shape, 1) < size // 2
                a_full[:levels, :] = jnp.zeros((levels, size), F32)
                a_full[levels : levels + rows, :] = jnp.where(
                    on_left, a, pltpu.roll(b, size // 2, 1)
                )
                a_full[levels + rows :, :] = jnp.where(
                    on_left, pltpu.roll(a, size // 2, 1), b
                )
                for k in range(window + 1):
                    level = base + k - 1
                    row = pl.ds(pl.multiple_of((level + 1) * levels, levels), levels)
                    a_win[which, t, k * levels : (k + 1) * levels, :] = a_full[row, :]
                    if k:
                        w_win[which, t, k - 1 : k, :] = ops[
                            which,
                            level // lev_dev,
                            pl.ds(rows + lax.rem(level, lev_dev) * tiles_dev + t, 1),
                            :,
                        ]

    for level in range(lev_dev):
        for t in range(tiles_dev):
            if level == t == 0:
                loads[0].wait()
            turned[level, t] = tracer[level, t * size : (t + 1) * size, :].T
    for q in range(Q):
        load_first(q)
    for load in loads[1:-1]:
        load.wait()
    pack()
    prepare_more()
    count = len(ALL) + has_ahead.astype(jnp.int32) + has_behind.astype(jnp.int32)
    pl.semaphore_wait(barrier, count)
    stage_a(0, 0)
    for q in range(1, Q):
        stage_a(0, q)
    for n in range(len(SAME)):
        ops_copy(n).start()
    pair = pair_copies()
    pair[0].start()
    loads[-1].wait()
    prepare()
    pair[1].start()
    stage_b(0, 0)
    pair[0].wait()
    positions()
    for q in range(1, Q):
        stage_b(0, q)
    pair[1].wait()
    stage_a(1, 0)
    for n in range(len(SAME)):
        ops_copy(n).wait()
    for copy in pass_copies():
        copy.start()
    stage_a(1, 1)
    stage_a(1, 2)
    for copy in pass_copies():
        copy.wait()
    operators()
    stage_a(1, 3)
    for late, p, q in ORDER:
        if late:
            stage_a(p + 1, q)
        else:
            stage_b(p, q)
    mine = lev_dev * v - base
    for q in range(Q):
        for t in range(tiles_dev):
            for level in range(lev_dev):
                final[part * Q + q, t, level] = halos[STEPS % 2 * Q + q][
                    blk + t * window + mine + level
                ]
    for q in range(Q):
        for copy in last_copies(q):
            copy.wait_recv()
    for level in range(lev_dev):
        for t in range(tiles_dev):
            whole = jnp.concatenate(
                [final[i, t, level] for i in range(2 * Q)], axis=0
            )
            out[level, t * size : (t + 1) * size, :] = whole.T
    for q in range(Q):
        for copy in step_copies(STEPS, q) + last_copies(q):
            copy.wait_send()


def on_device(h_size, v_size, tracer, tiles, columns, counts, source, implicit, settling, wet):
    lev_dev, cells_dev, classes = tracer.shape
    slots, size = tiles.shape[2], tiles.shape[3]
    tiles_dev = cells_dev // size
    levels = implicit.shape[1]
    share = implicit.shape[0]
    window = lev_dev + 2 * REACH
    assert lev_dev == 2 and tiles_dev == 2 and v_size == 4 and h_size % 2 == 0
    ch = classes // 2 // Q
    flat = implicit.reshape(share, levels * levels).T
    settling = settling.reshape(1, classes)
    extra = (levels * levels // 2 + 8, size)
    hbm = pl.BlockSpec(memory_space=pl.ANY)
    vm = pl.BlockSpec(memory_space=pltpu.VMEM)
    phases = STEPS + 1
    dma = pltpu.SemaphoreType.DMA
    return pl.pallas_call(
        functools.partial(kernel, h_size, v_size),
        out_shape=jax.ShapeDtypeStruct(tracer.shape, tracer.dtype),
        in_specs=[hbm] * 8,
        out_specs=vm,
        scratch_shapes=[
            pltpu.VMEM(tracer.shape, BF16),
            pltpu.VMEM(tiles.shape, BF16),
            pltpu.SMEM(counts.shape, jnp.int32),
            pltpu.VMEM(source.shape, BF16),
            pltpu.VMEM(flat.shape, F32),
            pltpu.VMEM(settling.shape, F32),
            pltpu.VMEM(wet.shape, jnp.int32),
            pltpu.VMEM(extra, F32),
            pltpu.VMEM((2 * lev_dev, tiles_dev, slots * size, size), BF16),
            pltpu.VMEM((lev_dev, tiles_dev, classes, size), BF16),
            pltpu.VMEM((2, Q, 2, levels, tiles_dev, ch, size), BF16),
            pltpu.VMEM((Q, lev_dev, tiles_dev, ch, size), BF16),
            pltpu.VMEM((2 * Q, tiles_dev, lev_dev, ch, size), BF16),
            pltpu.VMEM((tiles_dev, classes, size), F32),
            pltpu.VMEM((classes, size), F32),
            pltpu.VMEM((2, v_size) + extra, F32),
            pltpu.VMEM(((levels + 1) * levels, size), F32),
            pltpu.VMEM((2, tiles_dev, (window + 1) * levels, size), F32),
            pltpu.VMEM((2, tiles_dev, 8, size), F32),
            pltpu.VMEM((2,) + columns.shape, jnp.int32),
            pltpu.SMEM((2,) + columns.shape, jnp.int32),
            pltpu.SMEM((2 * lev_dev, tiles_dev * slots), jnp.int32),
            dma((phases, Q, 4)),
            dma((phases, Q, 4)),
            dma((Q, len(ALL))),
            dma((Q, len(ALL))),
            dma((Q, tiles_dev)),
            dma((Q, tiles_dev)),
            dma((len(SAME),)),
            dma((len(SAME),)),
            dma((2, 2)),
            dma((2, 2)),
            dma((2,)),
            dma((2,)),
            dma(()),
            dma((8,)),
        ]
        + [pltpu.VMEM((3 * tiles_dev * window, ch, size), BF16)] * (2 * Q),
        compiler_params=pltpu.CompilerParams(
            collective_id=0, has_side_effects=True, vmem_limit_bytes=32 * 2**20
        ),
    )(
        *(
            pltpu.with_memory_space_constraint(operand, pltpu.HBM)
            for operand in (
                tracer, tiles, columns, counts, source, flat, settling, wet
            )
        )
    )


def solution(mesh):
    placed = (
        P("vert", "horiz", None),
        P("vert", "horiz", None, None, None),
        P("vert", "horiz", None),
        P("vert", "horiz"),
        P("horiz", None),
        P(("horiz", "vert"), None, None),
        P(),
        P("vert", "horiz"),
    )
    body = functools.partial(on_device, mesh.shape["horiz"], mesh.shape["vert"])
    return jax.shard_map(
        body, mesh=mesh, in_specs=placed, out_specs=P("vert", "horiz", None), check_vma=False
    )
```

```python
import functools

import jax
import jax.numpy as jnp
from jax import lax
from jax.experimental import pallas as pl
from jax.experimental.pallas import tpu as pltpu
from jax.sharding import PartitionSpec as P

REACH = 2
STEPS = 4
Q = 4
ORDER = [
    (late, p, q)
    for when, late, p, q in sorted(
        (6.8 * p + 3.0 * late + 1.4 * q, late, p, q)
        for p in range(1, STEPS + 1)
        for late in range(2)
        for q in range(Q)
        if p + late <= STEPS
    )
]
MESH = pl.DeviceIdType.MESH
ALL = ((1, 1, 0), (1, 1, 1), (1, 0, 0), (1, 0, 1), (0, 1, 0), (0, 1, 1), (0, 0, 1))
SAME = ((1, 1, 1), (1, 0, 0), (0, 1, 1))
F32 = jnp.float32
BF16 = jnp.bfloat16


def kernel(
    h_size,
    v_size,
    tracer_hbm,
    tiles_hbm,
    columns_hbm,
    counts_hbm,
    source_hbm,
    flat_hbm,
    settling_hbm,
    wet_hbm,
    out,
    tracer,
    tiles,
    counts,
    source,
    flat,
    settling,
    wet,
    extra,
    weights,
    turned,
    gath,
    other,
    final,
    src_t,
    fall,
    ops,
    a_full,
    a_win,
    w_win,
    cols_v,
    cols_s,
    pos,
    send_sem,
    recv_sem,
    first_send,
    first_recv,
    last_send,
    last_recv,
    ops_send,
    ops_recv,
    pass_send,
    pass_recv,
    pair_send,
    pair_recv,
    local_sem,
    load_sem,
    *halos,
):
    lev_dev, cells_dev, classes = tracer.shape
    slots, size = tiles.shape[2], tiles.shape[3]
    tiles_dev = cells_dev // size
    window = lev_dev + 2 * REACH
    levels = lev_dev * v_size
    lev_chip = 2 * lev_dev
    h_tiles = h_size * tiles_dev
    half = classes // 2
    ch = half // Q
    blk = tiles_dev * window
    h = lax.axis_index("horiz")
    v = lax.axis_index("vert")
    even = lax.rem(h, 2) == 0
    core = lax.rem(v, 2)
    chip = v // 2
    base = 2 * chip
    partner = jnp.where(even, h + 1, h - 1)
    ahead = jnp.where(even, h + 2, h - 2)
    behind = jnp.where(even, h - 2, h + 2)
    has_ahead = (ahead >= 0) & (ahead < h_size)
    has_behind = (behind >= 0) & (behind < h_size)
    part = lax.rem(core + chip + h // 2, 2)
    central = lax.rem(core + chip, 2) == 1

    def target(dy, dx, dc):
        flipped = v
        if dc:
            flipped = flipped + 1 - 2 * core
        if dx:
            flipped = lax.rem(flipped + 2, 4)
        return {"horiz": partner if dy else h, "vert": flipped}

    def vert(d):
        return target(0, d // 2, d % 2)

    crossed = v + 1 - 2 * core
    front = {"horiz": ahead, "vert": crossed}
    back = {"horiz": behind, "vert": crossed}

    barrier = pltpu.get_barrier_semaphore()
    for dy, dx, dc in ALL:
        pl.semaphore_signal(
            barrier, inc=1, device_id=target(dy, dx, dc), device_id_type=MESH
        )

    @pl.when(has_ahead)
    def _():
        pl.semaphore_signal(barrier, inc=1, device_id=front, device_id_type=MESH)

    @pl.when(has_behind)
    def _():
        pl.semaphore_signal(barrier, inc=1, device_id=back, device_id_type=MESH)

    loads = [
        pltpu.make_async_copy(src, dst, load_sem.at[n])
        for n, (src, dst) in enumerate(
            (
                (tracer_hbm, tracer),
                (columns_hbm, cols_v.at[core]),
                (flat_hbm, flat),
                (wet_hbm, wet),
                (counts_hbm, counts),
                (settling_hbm, settling),
                (source_hbm, source),
                (tiles_hbm, tiles),
            )
        )
    ]
    for load in loads:
        load.start()

    near_at = jnp.where(even, 2 * blk, 0)
    far_at = jnp.where(even, 0, 2 * blk)

    def copy_to(src, dst, send, recv, where):
        return pltpu.make_async_remote_copy(
            src_ref=src,
            dst_ref=dst,
            send_sem=send,
            recv_sem=recv,
            device_id=where,
            device_id_type=MESH,
        )

    def remote(src, dst, p, q, kind, where):
        return copy_to(
            src, dst, send_sem.at[p, q, kind], recv_sem.at[p, q, kind], where
        )

    def first_copy(q, n):
        dy, dx, dc = ALL[n]
        mine = gath.at[0, q, 0, pl.ds(lev_dev * v, lev_dev)]
        return copy_to(
            other.at[q] if (dx + dc) % 2 else mine,
            gath.at[0, q, dy, pl.ds(lev_dev * v, lev_dev)],
            first_send.at[q, n],
            first_recv.at[q, n],
            target(dy, dx, dc),
        )

    def first_all(q, sending, act):
        for n, (dy, dx, dc) in enumerate(ALL):
            if not dx:
                act(first_copy(q, n))
                continue
            wanted = central if sending or dc else ~central

            @pl.when(wanted)
            def _():
                act(first_copy(q, n))

    def step_copy(p, q, n):
        dy, dx, dc = SAME[n]
        mine = gath.at[p % 2, q, 0, pl.ds(lev_chip * chip, lev_chip)]
        theirs = gath.at[p % 2, q, dy, pl.ds(lev_chip * chip, lev_chip)]
        return remote(mine, theirs, p, q, n, target(dy, dx, dc))

    def step_copies(p, q):
        kinds = (2,) if p == STEPS else (0, 2, 1)
        return [step_copy(p, q, n) for n in kinds]

    def block(p, q, at):
        return halos[p % 2 * Q + q].at[pl.ds(at, blk)]

    def front_copy(p, q):
        return remote(block(p, q, near_at), block(p, q, far_at), p, q, 3, front)

    def last_copies(q):
        theirs = lev_dev * (v + 1 - 2 * core) - base
        halo = halos[STEPS % 2 * Q + q]
        return [
            copy_to(
                halo.at[pl.ds(blk + t * window + theirs, lev_dev)],
                final.at[part * Q + q, t],
                last_send.at[q, t],
                last_recv.at[q, t],
                vert(1),
            )
            for t in range(tiles_dev)
        ]

    def pair_copies():
        mine = weights.at[pl.ds(lev_dev * core, lev_dev)]
        cols = cols_v.at[core]
        return [
            copy_to(cols, cols, pair_send.at[0], pair_recv.at[0], vert(1)),
            copy_to(mine, mine, pair_send.at[1], pair_recv.at[1], vert(1)),
        ]

    def load_first(q):
        for level in range(lev_dev):
            for t in range(tiles_dev):
                ours = pl.ds(pl.multiple_of(part * half + q * ch, ch), ch)
                theirs = pl.ds(pl.multiple_of((1 - part) * half + q * ch, ch), ch)
                gath[0, q, 0, lev_dev * v + level, t] = turned[level, t, ours, :]
                other[q, level, t] = turned[level, t, theirs, :]

    def explicit(p, q):
        for level in range(lev_chip):
            for t in range(tiles_dev):
                picked = jnp.concatenate(
                    [
                        halos[(p - 1) % 2 * Q + q][pos[level, t * slots + j]]
                        for j in range(slots)
                    ],
                    axis=1,
                )
                flow = jnp.dot(
                    picked, weights[level, t], preferred_element_type=F32
                )
                if level == 0:
                    ours = pl.ds(pl.multiple_of(part * half + q * ch, ch), ch)
                    flow = flow + src_t[t, ours, :]
                gath[p % 2, q, 0, lev_chip * chip + level, t] = flow.astype(BF16)

    def stage_a(p, q):
        if p == 0:
            first_all(q, True, lambda copy: copy.start())
            return
        if p > 1:
            solve_own(p - 1, q)
        if p == 1:
            first_all(q, True, lambda copy: copy.wait_send())
        else:
            for copy in step_copies(p - 1, q):
                copy.wait_send()

        @pl.when(has_behind)
        def _():
            front_copy(p - 1, q).wait_recv()

        explicit(p, q)
        for copy in step_copies(p, q):
            copy.start()

    def solve(p, q, which):
        par = p % 2
        halo = halos[par * Q + q]
        at0 = near_at if which else blk
        if p == 0:
            for t in range(tiles_dev):
                for k in range(window):
                    halo[at0 + t * window + k] = gath[par, q, which, base + k, t]
            return
        rows = 16

        for t in range(tiles_dev):
            for i in range(ch // rows):
                at = slice(i * rows, (i + 1) * rows)
                loaded = [
                    gath[par, q, which, m, t, at, :].astype(F32) for m in range(levels)
                ]
                start = part * half + q * ch + i * rows
                rate = fall[pl.ds(pl.multiple_of(start, rows), rows), :]
                stay = 1.0 - rate
                above = None
                for k in range(window + 1):
                    mixed = None
                    for m in range(levels):
                        r = k * levels + m
                        term = a_win[which, t, r : r + 1, :] * loaded[m]
                        mixed = term if m == 0 else mixed + term
                    if k:
                        settled = stay * mixed + rate * above
                        wet = w_win[which, t, k - 1 : k, :]
                        halo[at0 + t * window + k - 1, at, :] = (wet * settled).astype(
                            BF16
                        )
                    above = mixed

    def solve_own(p, q):
        if p:
            step_copy(p, q, 2).wait_recv()
        solve(p, q, 0)

    def stage_b(p, q):
        if p == 0:
            first_all(q, False, lambda copy: copy.wait_recv())
        elif p < STEPS:
            step_copy(p, q, 0).wait_recv()
            step_copy(p, q, 1).wait_recv()
        if p:

            @pl.when(has_ahead)
            def _():
                front_copy(p - 1, q).wait_send()

        if p < STEPS:
            solve(p, q, 1)

            @pl.when(has_ahead)
            def _():
                front_copy(p, q).start()

        if p == 0 or p == STEPS:
            solve_own(p, q)
        if p == STEPS:
            for copy in last_copies(q):
                copy.start()

    def ops_copy(n):
        dy, dx, dc = SAME[n]
        return copy_to(
            extra, ops.at[dy, v], ops_send.at[n], ops_recv.at[n], target(dy, dx, dc)
        )

    def pass_copies():
        across = v_size - 1 - v
        return [
            copy_to(
                ops.at[dy, at],
                ops.at[dy, at],
                pass_send.at[dy, n],
                pass_recv.at[dy, n],
                vert(1),
            )
            for dy in range(2)
            for n, at in enumerate((v, across))
        ]

    def pack():
        rows = levels * levels // 2
        extra[:rows, :] = jnp.concatenate([flat[:rows, :], flat[rows:, :]], axis=1)
        extra[rows:, :] = jnp.zeros((8, size), F32)
        for level in range(lev_dev):
            for t in range(tiles_dev):
                at = rows + level * tiles_dev + t
                extra[at : at + 1, :] = wet[
                    level : level + 1, t * size : (t + 1) * size
                ].astype(F32)
        ops[0, v] = extra[...]

    def prepare():
        for level in range(lev_dev):
            for t in range(tiles_dev):
                for j in range(slots):
                    live = (j < counts[level, t]).astype(F32)
                    weights[lev_dev * core + level, t, j * size : (j + 1) * size, :] = (
                        tiles[level, t, j].astype(F32).T * live
                    ).astype(BF16)

    def prepare_more():
        on_top = (chip == 0).astype(F32)
        for t in range(tiles_dev):
            src_t[t] = source[t * size : (t + 1) * size, :].astype(F32).T * on_top
        fall[...] = jnp.broadcast_to(settling[...], (size, classes)).T

    def positions():
        local = pltpu.make_async_copy(cols_v, cols_s, local_sem)
        local.start()
        local.wait()
        last = 3 * blk - 1
        for level in range(lev_chip):
            for n in range(tiles_dev * slots):
                column = cols_s[
                    level // lev_dev, level % lev_dev, n // slots, n % slots
                ]
                row = lax.div(column, h_tiles) - base
                across = lax.rem(column, h_tiles) - tiles_dev * h + REACH
                pos[level, n] = jnp.clip(across * window + row, 0, last)

    def operators():
        rows = levels * levels // 2
        for which in range(2):
            for t in range(tiles_dev):
                a = ops[which, 2 * t, :rows, :]
                b = ops[which, 2 * t + 1, :rows, :]
                on_left = lax.broadcasted_iota(jnp.int32, a.shape, 1) < size // 2
                a_full[:levels, :] = jnp.zeros((levels, size), F32)
                a_full[levels : levels + rows, :] = jnp.where(
                    on_left, a, pltpu.roll(b, size // 2, 1)
                )
                a_full[levels + rows :, :] = jnp.where(
                    on_left, pltpu.roll(a, size // 2, 1), b
                )
                for k in range(window + 1):
                    level = base + k - 1
                    row = pl.ds(pl.multiple_of((level + 1) * levels, levels), levels)
                    a_win[which, t, k * levels : (k + 1) * levels, :] = a_full[row, :]
                    if k:
                        w_win[which, t, k - 1 : k, :] = ops[
                            which,
                            level // lev_dev,
                            pl.ds(rows + lax.rem(level, lev_dev) * tiles_dev + t, 1),
                            :,
                        ]

    for level in range(lev_dev):
        for t in range(tiles_dev):
            if level == t == 0:
                loads[0].wait()
            turned[level, t] = tracer[level, t * size : (t + 1) * size, :].T
    for q in range(Q):
        load_first(q)
    for load in loads[1:-1]:
        load.wait()
    pack()
    prepare_more()
    count = len(ALL) + has_ahead.astype(jnp.int32) + has_behind.astype(jnp.int32)
    pl.semaphore_wait(barrier, count)
    stage_a(0, 0)
    for q in range(1, Q):
        stage_a(0, q)
    for n in range(len(SAME)):
        ops_copy(n).start()
    pair = pair_copies()
    pair[0].start()
    loads[-1].wait()
    prepare()
    pair[1].start()
    stage_b(0, 0)
    pair[0].wait()
    positions()
    for q in range(1, Q):
        stage_b(0, q)
    pair[1].wait()
    stage_a(1, 0)
    for n in range(len(SAME)):
        ops_copy(n).wait()
    for copy in pass_copies():
        copy.start()
    stage_a(1, 1)
    stage_a(1, 2)
    for copy in pass_copies():
        copy.wait()
    operators()
    stage_a(1, 3)
    for late, p, q in ORDER:
        if late:
            stage_a(p + 1, q)
        else:
            stage_b(p, q)
    mine = lev_dev * v - base
    for q in range(Q):
        for t in range(tiles_dev):
            for level in range(lev_dev):
                final[part * Q + q, t, level] = halos[STEPS % 2 * Q + q][
                    blk + t * window + mine + level
                ]
    for q in range(Q):
        for copy in last_copies(q):
            copy.wait_recv()
    for level in range(lev_dev):
        for t in range(tiles_dev):
            whole = jnp.concatenate(
                [final[i, t, level] for i in range(2 * Q)], axis=0
            )
            out[level, t * size : (t + 1) * size, :] = whole.T
    for q in range(Q):
        for copy in step_copies(STEPS, q) + last_copies(q):
            copy.wait_send()


def on_device(h_size, v_size, tracer, tiles, columns, counts, source, implicit, settling, wet):
    lev_dev, cells_dev, classes = tracer.shape
    slots, size = tiles.shape[2], tiles.shape[3]
    tiles_dev = cells_dev // size
    levels = implicit.shape[1]
    share = implicit.shape[0]
    window = lev_dev + 2 * REACH
    assert lev_dev == 2 and tiles_dev == 2 and v_size == 4 and h_size % 2 == 0
    ch = classes // 2 // Q
    flat = implicit.reshape(share, levels * levels).T
    settling = settling.reshape(1, classes)
    extra = (levels * levels // 2 + 8, size)
    hbm = pl.BlockSpec(memory_space=pl.ANY)
    vm = pl.BlockSpec(memory_space=pltpu.VMEM)
    phases = STEPS + 1
    dma = pltpu.SemaphoreType.DMA
    return pl.pallas_call(
        functools.partial(kernel, h_size, v_size),
        out_shape=jax.ShapeDtypeStruct(tracer.shape, tracer.dtype),
        in_specs=[hbm] * 8,
        out_specs=vm,
        scratch_shapes=[
            pltpu.VMEM(tracer.shape, BF16),
            pltpu.VMEM(tiles.shape, BF16),
            pltpu.SMEM(counts.shape, jnp.int32),
            pltpu.VMEM(source.shape, BF16),
            pltpu.VMEM(flat.shape, F32),
            pltpu.VMEM(settling.shape, F32),
            pltpu.VMEM(wet.shape, jnp.int32),
            pltpu.VMEM(extra, F32),
            pltpu.VMEM((2 * lev_dev, tiles_dev, slots * size, size), BF16),
            pltpu.VMEM((lev_dev, tiles_dev, classes, size), BF16),
            pltpu.VMEM((2, Q, 2, levels, tiles_dev, ch, size), BF16),
            pltpu.VMEM((Q, lev_dev, tiles_dev, ch, size), BF16),
            pltpu.VMEM((2 * Q, tiles_dev, lev_dev, ch, size), BF16),
            pltpu.VMEM((tiles_dev, classes, size), F32),
            pltpu.VMEM((classes, size), F32),
            pltpu.VMEM((2, v_size) + extra, F32),
            pltpu.VMEM(((levels + 1) * levels, size), F32),
            pltpu.VMEM((2, tiles_dev, (window + 1) * levels, size), F32),
            pltpu.VMEM((2, tiles_dev, 8, size), F32),
            pltpu.VMEM((2,) + columns.shape, jnp.int32),
            pltpu.SMEM((2,) + columns.shape, jnp.int32),
            pltpu.SMEM((2 * lev_dev, tiles_dev * slots), jnp.int32),
            dma((phases, Q, 4)),
            dma((phases, Q, 4)),
            dma((Q, len(ALL))),
            dma((Q, len(ALL))),
            dma((Q, tiles_dev)),
            dma((Q, tiles_dev)),
            dma((len(SAME),)),
            dma((len(SAME),)),
            dma((2, 2)),
            dma((2, 2)),
            dma((2,)),
            dma((2,)),
            dma(()),
            dma((8,)),
        ]
        + [pltpu.VMEM((3 * tiles_dev * window, ch, size), BF16)] * (2 * Q),
        compiler_params=pltpu.CompilerParams(
            collective_id=0, has_side_effects=True, vmem_limit_bytes=32 * 2**20
        ),
    )(
        *(
            pltpu.with_memory_space_constraint(operand, pltpu.HBM)
            for operand in (
                tracer, tiles, columns, counts, source, flat, settling, wet
            )
        )
    )


def solution(mesh):
    placed = (
        P("vert", "horiz", None),
        P("vert", "horiz", None, None, None),
        P("vert", "horiz", None),
        P("vert", "horiz"),
        P("horiz", None),
        P(("horiz", "vert"), None, None),
        P(),
        P("vert", "horiz"),
    )
    body = functools.partial(on_device, mesh.shape["horiz"], mesh.shape["vert"])
    return jax.shard_map(
        body, mesh=mesh, in_specs=placed, out_specs=P("vert", "horiz", None), check_vma=False
    )
```

```python
import functools

import jax
import jax.numpy as jnp
from jax import lax
from jax.experimental import pallas as pl
from jax.experimental.pallas import tpu as pltpu
from jax.sharding import PartitionSpec as P

REACH = 2
STEPS = 4
Q = 4
ORDER = [
    (late, p, q)
    for when, late, p, q in sorted(
        (6.8 * p + 3.0 * late + 1.4 * q, late, p, q)
        for p in range(1, STEPS + 1)
        for late in range(2)
        for q in range(Q)
        if p + late <= STEPS
    )
]
MESH = pl.DeviceIdType.MESH
ALL = ((1, 1, 0), (1, 1, 1), (1, 0, 0), (1, 0, 1), (0, 1, 0), (0, 1, 1), (0, 0, 1))
SAME = ((1, 1, 1), (1, 0, 0), (0, 1, 1))
F32 = jnp.float32
BF16 = jnp.bfloat16


def kernel(
    h_size,
    v_size,
    tracer_hbm,
    tiles_hbm,
    columns_hbm,
    counts_hbm,
    source_hbm,
    flat_hbm,
    settling_hbm,
    wet_hbm,
    out,
    tracer,
    tiles,
    counts,
    source,
    flat,
    settling,
    wet,
    extra,
    weights,
    turned,
    gath,
    other,
    final,
    src_t,
    fall,
    ops,
    a_full,
    a_win,
    w_win,
    cols_v,
    cols_s,
    pos,
    send_sem,
    recv_sem,
    first_send,
    first_recv,
    last_send,
    last_recv,
    ops_send,
    ops_recv,
    pass_send,
    pass_recv,
    pair_send,
    pair_recv,
    local_sem,
    load_sem,
    *halos,
):
    lev_dev, cells_dev, classes = tracer.shape
    slots, size = tiles.shape[2], tiles.shape[3]
    tiles_dev = cells_dev // size
    window = lev_dev + 2 * REACH
    levels = lev_dev * v_size
    lev_chip = 2 * lev_dev
    h_tiles = h_size * tiles_dev
    half = classes // 2
    ch = half // Q
    blk = tiles_dev * window
    h = lax.axis_index("horiz")
    v = lax.axis_index("vert")
    even = lax.rem(h, 2) == 0
    core = lax.rem(v, 2)
    chip = v // 2
    base = 2 * chip
    partner = jnp.where(even, h + 1, h - 1)
    ahead = jnp.where(even, h + 2, h - 2)
    behind = jnp.where(even, h - 2, h + 2)
    has_ahead = (ahead >= 0) & (ahead < h_size)
    has_behind = (behind >= 0) & (behind < h_size)
    part = lax.rem(core + chip + h // 2, 2)
    central = lax.rem(core + chip, 2) == 1

    def target(dy, dx, dc):
        flipped = v
        if dc:
            flipped = flipped + 1 - 2 * core
        if dx:
            flipped = lax.rem(flipped + 2, 4)
        return {"horiz": partner if dy else h, "vert": flipped}

    def vert(d):
        return target(0, d // 2, d % 2)

    crossed = v + 1 - 2 * core
    front = {"horiz": ahead, "vert": crossed}
    back = {"horiz": behind, "vert": crossed}

    barrier = pltpu.get_barrier_semaphore()
    for dy, dx, dc in ALL:
        pl.semaphore_signal(
            barrier, inc=1, device_id=target(dy, dx, dc), device_id_type=MESH
        )

    @pl.when(has_ahead)
    def _():
        pl.semaphore_signal(barrier, inc=1, device_id=front, device_id_type=MESH)

    @pl.when(has_behind)
    def _():
        pl.semaphore_signal(barrier, inc=1, device_id=back, device_id_type=MESH)

    loads = [
        pltpu.make_async_copy(src, dst, load_sem.at[n])
        for n, (src, dst) in enumerate(
            (
                (tracer_hbm, tracer),
                (columns_hbm, cols_v.at[core]),
                (flat_hbm, flat),
                (wet_hbm, wet),
                (counts_hbm, counts),
                (settling_hbm, settling),
                (source_hbm, source),
                (tiles_hbm, tiles),
            )
        )
    ]
    for load in loads:
        load.start()

    near_at = jnp.where(even, 2 * blk, 0)
    far_at = jnp.where(even, 0, 2 * blk)

    def copy_to(src, dst, send, recv, where):
        return pltpu.make_async_remote_copy(
            src_ref=src,
            dst_ref=dst,
            send_sem=send,
            recv_sem=recv,
            device_id=where,
            device_id_type=MESH,
        )

    def remote(src, dst, p, q, kind, where):
        return copy_to(
            src, dst, send_sem.at[p, q, kind], recv_sem.at[p, q, kind], where
        )

    def first_copy(q, n):
        dy, dx, dc = ALL[n]
        mine = gath.at[0, q, 0, pl.ds(lev_dev * v, lev_dev)]
        return copy_to(
            other.at[q] if (dx + dc) % 2 else mine,
            gath.at[0, q, dy, pl.ds(lev_dev * v, lev_dev)],
            first_send.at[q, n],
            first_recv.at[q, n],
            target(dy, dx, dc),
        )

    def first_all(q, sending, act):
        for n, (dy, dx, dc) in enumerate(ALL):
            if not dx:
                act(first_copy(q, n))
                continue
            wanted = central if sending or dc else ~central

            @pl.when(wanted)
            def _():
                act(first_copy(q, n))

    def step_copy(p, q, n):
        dy, dx, dc = SAME[n]
        mine = gath.at[p % 2, q, 0, pl.ds(lev_chip * chip, lev_chip)]
        theirs = gath.at[p % 2, q, dy, pl.ds(lev_chip * chip, lev_chip)]
        return remote(mine, theirs, p, q, n, target(dy, dx, dc))

    def step_copies(p, q):
        kinds = (2,) if p == STEPS else (0, 2, 1)
        return [step_copy(p, q, n) for n in kinds]

    def block(p, q, at):
        return halos[p % 2 * Q + q].at[pl.ds(at, blk)]

    def front_copy(p, q):
        return remote(block(p, q, near_at), block(p, q, far_at), p, q, 3, front)

    def last_copies(q):
        theirs = lev_dev * (v + 1 - 2 * core) - base
        halo = halos[STEPS % 2 * Q + q]
        return [
            copy_to(
                halo.at[pl.ds(blk + t * window + theirs, lev_dev)],
                final.at[part * Q + q, t],
                last_send.at[q, t],
                last_recv.at[q, t],
                vert(1),
            )
            for t in range(tiles_dev)
        ]

    def pair_copies():
        mine = weights.at[pl.ds(lev_dev * core, lev_dev)]
        cols = cols_v.at[core]
        return [
            copy_to(cols, cols, pair_send.at[0], pair_recv.at[0], vert(1)),
            copy_to(mine, mine, pair_send.at[1], pair_recv.at[1], vert(1)),
        ]

    def load_first(q):
        for level in range(lev_dev):
            for t in range(tiles_dev):
                ours = pl.ds(pl.multiple_of(part * half + q * ch, ch), ch)
                theirs = pl.ds(pl.multiple_of((1 - part) * half + q * ch, ch), ch)
                gath[0, q, 0, lev_dev * v + level, t] = turned[level, t, ours, :]
                other[q, level, t] = turned[level, t, theirs, :]

    def explicit(p, q):
        for level in range(lev_chip):
            for t in range(tiles_dev):
                picked = jnp.concatenate(
                    [
                        halos[(p - 1) % 2 * Q + q][pos[level, t * slots + j]]
                        for j in range(slots)
                    ],
                    axis=1,
                )
                flow = jnp.dot(
                    picked, weights[level, t], preferred_element_type=F32
                )
                if level == 0:
                    ours = pl.ds(pl.multiple_of(part * half + q * ch, ch), ch)
                    flow = flow + src_t[t, ours, :]
                gath[p % 2, q, 0, lev_chip * chip + level, t] = flow.astype(BF16)

    def stage_a(p, q):
        if p == 0:
            first_all(q, True, lambda copy: copy.start())
            return
        if p > 1:
            solve_own(p - 1, q)
        if p == 1:
            first_all(q, True, lambda copy: copy.wait_send())
        else:
            for copy in step_copies(p - 1, q):
                copy.wait_send()

        @pl.when(has_behind)
        def _():
            front_copy(p - 1, q).wait_recv()

        explicit(p, q)
        for copy in step_copies(p, q):
            copy.start()

    def solve(p, q, which):
        par = p % 2
        halo = halos[par * Q + q]
        at0 = near_at if which else blk
        if p == 0:
            for t in range(tiles_dev):
                for k in range(window):
                    halo[at0 + t * window + k] = gath[par, q, which, base + k, t]
            return
        rows = 16

        for t in range(tiles_dev):
            for i in range(ch // rows):
                at = slice(i * rows, (i + 1) * rows)
                loaded = [
                    gath[par, q, which, m, t, at, :].astype(F32) for m in range(levels)
                ]
                start = part * half + q * ch + i * rows
                rate = fall[pl.ds(pl.multiple_of(start, rows), rows), :]
                stay = 1.0 - rate
                above = None
                for k in range(window + 1):
                    mixed = None
                    for m in range(levels):
                        r = k * levels + m
                        term = a_win[which, t, r : r + 1, :] * loaded[m]
                        mixed = term if m == 0 else mixed + term
                    if k:
                        settled = stay * mixed + rate * above
                        wet = w_win[which, t, k - 1 : k, :]
                        halo[at0 + t * window + k - 1, at, :] = (wet * settled).astype(
                            BF16
                        )
                    above = mixed

    def solve_own(p, q):
        if p:
            step_copy(p, q, 2).wait_recv()
        solve(p, q, 0)

    def stage_b(p, q):
        if p == 0:
            first_all(q, False, lambda copy: copy.wait_recv())
        elif p < STEPS:
            step_copy(p, q, 0).wait_recv()
            step_copy(p, q, 1).wait_recv()
        if p:

            @pl.when(has_ahead)
            def _():
                front_copy(p - 1, q).wait_send()

        if p < STEPS:
            solve(p, q, 1)

            @pl.when(has_ahead)
            def _():
                front_copy(p, q).start()

        if p == 0 or p == STEPS:
            solve_own(p, q)
        if p == STEPS:
            for copy in last_copies(q):
                copy.start()

    def ops_copy(n):
        dy, dx, dc = SAME[n]
        return copy_to(
            extra, ops.at[dy, v], ops_send.at[n], ops_recv.at[n], target(dy, dx, dc)
        )

    def pass_copies():
        across = v_size - 1 - v
        return [
            copy_to(
                ops.at[dy, at],
                ops.at[dy, at],
                pass_send.at[dy, n],
                pass_recv.at[dy, n],
                vert(1),
            )
            for dy in range(2)
            for n, at in enumerate((v, across))
        ]

    def pack():
        rows = levels * levels // 2
        extra[:rows, :] = jnp.concatenate([flat[:rows, :], flat[rows:, :]], axis=1)
        extra[rows:, :] = jnp.zeros((8, size), F32)
        for level in range(lev_dev):
            for t in range(tiles_dev):
                at = rows + level * tiles_dev + t
                extra[at : at + 1, :] = wet[
                    level : level + 1, t * size : (t + 1) * size
                ].astype(F32)
        ops[0, v] = extra[...]

    def prepare():
        for level in range(lev_dev):
            for t in range(tiles_dev):
                for j in range(slots):
                    live = (j < counts[level, t]).astype(F32)
                    weights[lev_dev * core + level, t, j * size : (j + 1) * size, :] = (
                        tiles[level, t, j].astype(F32).T * live
                    ).astype(BF16)

    def prepare_more():
        on_top = (chip == 0).astype(F32)
        for t in range(tiles_dev):
            src_t[t] = source[t * size : (t + 1) * size, :].astype(F32).T * on_top
        fall[...] = jnp.broadcast_to(settling[...], (size, classes)).T

    def positions():
        local = pltpu.make_async_copy(cols_v, cols_s, local_sem)
        local.start()
        local.wait()
        last = 3 * blk - 1
        for level in range(lev_chip):
            for n in range(tiles_dev * slots):
                column = cols_s[
                    level // lev_dev, level % lev_dev, n // slots, n % slots
                ]
                row = lax.div(column, h_tiles) - base
                across = lax.rem(column, h_tiles) - tiles_dev * h + REACH
                pos[level, n] = jnp.clip(across * window + row, 0, last)

    def operators():
        rows = levels * levels // 2
        for which in range(2):
            for t in range(tiles_dev):
                a = ops[which, 2 * t, :rows, :]
                b = ops[which, 2 * t + 1, :rows, :]
                on_left = lax.broadcasted_iota(jnp.int32, a.shape, 1) < size // 2
                a_full[:levels, :] = jnp.zeros((levels, size), F32)
                a_full[levels : levels + rows, :] = jnp.where(
                    on_left, a, pltpu.roll(b, size // 2, 1)
                )
                a_full[levels + rows :, :] = jnp.where(
                    on_left, pltpu.roll(a, size // 2, 1), b
                )
                for k in range(window + 1):
                    level = base + k - 1
                    row = pl.ds(pl.multiple_of((level + 1) * levels, levels), levels)
                    a_win[which, t, k * levels : (k + 1) * levels, :] = a_full[row, :]
                    if k:
                        w_win[which, t, k - 1 : k, :] = ops[
                            which,
                            level // lev_dev,
                            pl.ds(rows + lax.rem(level, lev_dev) * tiles_dev + t, 1),
                            :,
                        ]

    for level in range(lev_dev):
        for t in range(tiles_dev):
            if level == t == 0:
                loads[0].wait()
            turned[level, t] = tracer[level, t * size : (t + 1) * size, :].T
    for q in range(Q):
        load_first(q)
    for load in loads[1:-1]:
        load.wait()
    pack()
    prepare_more()
    loads[-1].wait()
    prepare()
    count = len(ALL) + has_ahead.astype(jnp.int32) + has_behind.astype(jnp.int32)
    pl.semaphore_wait(barrier, count)
    stage_a(0, 0)
    for q in range(1, Q):
        stage_a(0, q)
    for n in range(len(SAME)):
        ops_copy(n).start()
    pair = pair_copies()
    pair[0].start()
    pair[1].start()
    stage_b(0, 0)
    pair[0].wait()
    positions()
    for q in range(1, Q):
        stage_b(0, q)
    pair[1].wait()
    stage_a(1, 0)
    for n in range(len(SAME)):
        ops_copy(n).wait()
    for copy in pass_copies():
        copy.start()
    stage_a(1, 1)
    stage_a(1, 2)
    for copy in pass_copies():
        copy.wait()
    operators()
    stage_a(1, 3)
    for late, p, q in ORDER:
        if late:
            stage_a(p + 1, q)
        else:
            stage_b(p, q)
    mine = lev_dev * v - base
    for q in range(Q):
        for t in range(tiles_dev):
            for level in range(lev_dev):
                final[part * Q + q, t, level] = halos[STEPS % 2 * Q + q][
                    blk + t * window + mine + level
                ]
    for q in range(Q):
        for copy in last_copies(q):
            copy.wait_recv()
    for level in range(lev_dev):
        for t in range(tiles_dev):
            whole = jnp.concatenate(
                [final[i, t, level] for i in range(2 * Q)], axis=0
            )
            out[level, t * size : (t + 1) * size, :] = whole.T
    for q in range(Q):
        for copy in step_copies(STEPS, q) + last_copies(q):
            copy.wait_send()


def on_device(h_size, v_size, tracer, tiles, columns, counts, source, implicit, settling, wet):
    lev_dev, cells_dev, classes = tracer.shape
    slots, size = tiles.shape[2], tiles.shape[3]
    tiles_dev = cells_dev // size
    levels = implicit.shape[1]
    share = implicit.shape[0]
    window = lev_dev + 2 * REACH
    assert lev_dev == 2 and tiles_dev == 2 and v_size == 4 and h_size % 2 == 0
    ch = classes // 2 // Q
    flat = implicit.reshape(share, levels * levels).T
    settling = settling.reshape(1, classes)
    extra = (levels * levels // 2 + 8, size)
    hbm = pl.BlockSpec(memory_space=pl.ANY)
    vm = pl.BlockSpec(memory_space=pltpu.VMEM)
    phases = STEPS + 1
    dma = pltpu.SemaphoreType.DMA
    return pl.pallas_call(
        functools.partial(kernel, h_size, v_size),
        out_shape=jax.ShapeDtypeStruct(tracer.shape, tracer.dtype),
        in_specs=[hbm] * 8,
        out_specs=vm,
        scratch_shapes=[
            pltpu.VMEM(tracer.shape, BF16),
            pltpu.VMEM(tiles.shape, BF16),
            pltpu.SMEM(counts.shape, jnp.int32),
            pltpu.VMEM(source.shape, BF16),
            pltpu.VMEM(flat.shape, F32),
            pltpu.VMEM(settling.shape, F32),
            pltpu.VMEM(wet.shape, jnp.int32),
            pltpu.VMEM(extra, F32),
            pltpu.VMEM((2 * lev_dev, tiles_dev, slots * size, size), BF16),
            pltpu.VMEM((lev_dev, tiles_dev, classes, size), BF16),
            pltpu.VMEM((2, Q, 2, levels, tiles_dev, ch, size), BF16),
            pltpu.VMEM((Q, lev_dev, tiles_dev, ch, size), BF16),
            pltpu.VMEM((2 * Q, tiles_dev, lev_dev, ch, size), BF16),
            pltpu.VMEM((tiles_dev, classes, size), F32),
            pltpu.VMEM((classes, size), F32),
            pltpu.VMEM((2, v_size) + extra, F32),
            pltpu.VMEM(((levels + 1) * levels, size), F32),
            pltpu.VMEM((2, tiles_dev, (window + 1) * levels, size), F32),
            pltpu.VMEM((2, tiles_dev, 8, size), F32),
            pltpu.VMEM((2,) + columns.shape, jnp.int32),
            pltpu.SMEM((2,) + columns.shape, jnp.int32),
            pltpu.SMEM((2 * lev_dev, tiles_dev * slots), jnp.int32),
            dma((phases, Q, 4)),
            dma((phases, Q, 4)),
            dma((Q, len(ALL))),
            dma((Q, len(ALL))),
            dma((Q, tiles_dev)),
            dma((Q, tiles_dev)),
            dma((len(SAME),)),
            dma((len(SAME),)),
            dma((2, 2)),
            dma((2, 2)),
            dma((2,)),
            dma((2,)),
            dma(()),
            dma((8,)),
        ]
        + [pltpu.VMEM((3 * tiles_dev * window, ch, size), BF16)] * (2 * Q),
        compiler_params=pltpu.CompilerParams(
            collective_id=0, has_side_effects=True, vmem_limit_bytes=32 * 2**20
        ),
    )(
        *(
            pltpu.with_memory_space_constraint(operand, pltpu.HBM)
            for operand in (
                tracer, tiles, columns, counts, source, flat, settling, wet
            )
        )
    )


def solution(mesh):
    placed = (
        P("vert", "horiz", None),
        P("vert", "horiz", None, None, None),
        P("vert", "horiz", None),
        P("vert", "horiz"),
        P("horiz", None),
        P(("horiz", "vert"), None, None),
        P(),
        P("vert", "horiz"),
    )
    body = functools.partial(on_device, mesh.shape["horiz"], mesh.shape["vert"])
    return jax.shard_map(
        body, mesh=mesh, in_specs=placed, out_specs=P("vert", "horiz", None), check_vma=False
    )
```
